32 devices in a mesh: req: 16 (over z, y, x), mlp: 2 (over core).
Axes of the slice: x: 2, y: 2, z: 4, core: 2. Of those that a mesh axis runs over, the one named last changes fastest.
Arguments:
- resid: bfloat16 [512, 2048], P('req'), may hold values from -50 to 50
- q_in: bfloat16 [512, 2048], P('req', 'mlp'), may hold values from -36 to 36
- kv_in: bfloat16 [512, 2, 512], P('req', None, 'mlp'), may hold values from -36 to 36
- parents: int32 [32, 16], P('req'), may hold values from -1 to 14, as said below
- counts: int32 [32], P('req'), may hold values from 8 to 16, as said below
- accept_leaf: int32 [32], P('req'), may hold values from 0 to 15, as said below
- cache: bfloat16 [1024, 2, 128, 512], P('req', None, None, 'mlp'), may hold values from -6 to 6
- held_table: int32 [32, 48], P('req'), may hold values from 0 to 63, as said below
- held_len: int32 [32], P('req'), may hold values from 1 to 6144, as said below
- prev_owner: int32 [16], P('req'), may hold values from 0 to 15, as said below
- w_out: bfloat16 [2048, 2048], P('mlp'), may hold values from -0.125 to 0.125
- gain_mid: bfloat16 [2048], replicated, may hold values from 0.099609375 to 1.8984375
- w_in: bfloat16 [2, 8192, 2048], P(None, ('req', 'mlp')), may hold values from -0.125 to 0.125
- w_down: bfloat16 [8192, 2048], P(('req', 'mlp')), may hold values from -0.0625 to 0.0625
- gain_next: bfloat16 [2048], replicated, may hold values from 0.099609375 to 1.8984375
- w_next: bfloat16 [2048, 3072], P(None, 'mlp'), may hold values from -0.125 to 0.125
Outputs:
- hidden_out: bfloat16 [512, 2048], P('req')
- next_qkv: bfloat16 [512, 3072], P('req', 'mlp')
- accepted_kv: bfloat16 [512, 2, 512], P('req', None, 'mlp')
The draws below stay inside these ranges and needn't reach their ends.
Inputs may be any that keep to these rules, and one draw needn't show every extreme that they name: parents[r, 0] is -1; for i of 1 or more parents[r, i] lies in 0 to i - 1. Draft tokens 0 to counts[r] - 1 of request r are live; some request has 16. `accept_leaf`: a live draft token of the request. `held_len`: entry 2 d holds the length of request 2 d, entry 2 d + 1 that of request 2 e + 1 where prev_owner[e] = d; some entry is 6144; the pages used by the two caches of one index of req are distinct. `held_table`: rows 2 d and 2 d + 1 belong to index d of req, as in held_len. `prev_owner`: one cycle through all indices of req, so never d itself.
All inputs are finite; a program needn't handle non-finite values.
Results may differ from the reference program's by a relative error of at most 0.014.
Values may be sent and summed in bfloat16 or wider, within the bound.
A program may use at most 128 MiB of HBM per device.

```python
import jax
import jax.numpy as jnp
from jax import lax

D = 2048
HEADS = 32
KV_HEADS = 8
HEAD_DIM = 64
FF = 8192
DRAFT = 16
PAGE = 128
MAXLEN = 6144
POOL = 64
GROUP = 4
QKV_WIDTH = 3072
MAXPAGES = 48
OWNERS = 16
REQS = 32
TOKENS = 512


def draw_q_in(key, part):
    shape = (REQS, DRAFT, KV_HEADS, HEADS // KV_HEADS, HEAD_DIM)
    base = jnp.clip(jax.random.normal(jax.random.fold_in(key, 1), shape, jnp.float32), -6.0, 6.0)
    return base.reshape(TOKENS, HEADS * HEAD_DIM).astype(jnp.bfloat16)


def draw_kv_in(key, part):
    shape = (REQS, DRAFT, 2, KV_HEADS, HEAD_DIM)
    base = jnp.clip(jax.random.normal(jax.random.fold_in(key, 2), shape, jnp.float32), -6.0, 6.0)
    return base.reshape(TOKENS, 2, KV_HEADS * HEAD_DIM).astype(jnp.bfloat16)


def draw_resid(key, part):
    row_scale = jnp.exp(jax.random.uniform(jax.random.fold_in(key, 31), (TOKENS, 1), jnp.float32, -1.2, 1.2))
    col_scale = jnp.exp(jax.random.uniform(jax.random.fold_in(key, 32), (1, D), jnp.float32, -1.2, 1.2))
    base = jnp.clip(jax.random.normal(jax.random.fold_in(key, 33), (TOKENS, D), jnp.float32), -4.0, 4.0)
    return (base * row_scale * col_scale).astype(jnp.bfloat16)


def draw_parents(key, part):
    nodes = jnp.arange(DRAFT, dtype=jnp.int32)
    picks = jax.random.randint(jax.random.fold_in(key, 3), (REQS, DRAFT), 0, 1 << 20)
    chosen = picks % jnp.maximum(nodes, 1)[None, :]
    return jnp.where(nodes[None, :] == 0, -1, chosen).astype(jnp.int32)


def draft_plan(key):
    requests = jnp.arange(REQS, dtype=jnp.int32)
    sizes = jax.random.randint(jax.random.fold_in(key, 5), (REQS,), DRAFT // 2, DRAFT + 1)
    widest = jax.random.randint(jax.random.fold_in(key, 6), (), 0, REQS)
    lowest_leaf = (widest + 1) % REQS
    fewest = (widest + 2) % REQS
    sizes = jnp.where(requests == widest, DRAFT, sizes)
    sizes = jnp.where(requests == fewest, DRAFT // 2, sizes)
    picks = jax.random.randint(jax.random.fold_in(key, 7), (REQS,), 0, 1 << 20)
    leaves = picks % sizes
    leaves = jnp.where(requests == widest, DRAFT - 1, leaves)
    leaves = jnp.where(requests == lowest_leaf, 0, leaves)
    return (sizes.astype(jnp.int32), leaves.astype(jnp.int32))


def draw_counts(key, part):
    return draft_plan(key)[0]


def draw_accept_leaf(key, part):
    return draft_plan(key)[1]


def shuffled_pages(key):
    return jax.random.permutation(key, POOL)


def pool_plan(key):
    expo = jax.random.randint(jax.random.fold_in(key, 11), (OWNERS, 2), 2, MAXLEN.bit_length())
    picks = jax.random.randint(jax.random.fold_in(key, 12), (OWNERS, 2), 0, 1 << 24)
    lengths = jnp.minimum(1 + picks % jnp.left_shift(jnp.int32(1), expo), MAXLEN)
    widest = jax.random.randint(jax.random.fold_in(key, 13), (), 0, OWNERS)
    wide_slot = jax.random.randint(jax.random.fold_in(key, 14), (), 0, 2)
    owners_row = jnp.arange(OWNERS, dtype=jnp.int32)[:, None]
    slot_col = jnp.arange(2, dtype=jnp.int32)[None, :]
    lengths = jnp.where((owners_row == widest) & (slot_col == wide_slot), MAXLEN, lengths)
    first = lengths[:, 0]
    first = jnp.where((jnp.arange(OWNERS, dtype=jnp.int32) == widest) & (wide_slot == 1), jnp.minimum(first, POOL * PAGE - MAXLEN), first)
    first_pages = (first + PAGE - 1) // PAGE
    second = jnp.minimum(lengths[:, 1], POOL * PAGE - first_pages * PAGE)
    orders = jax.vmap(shuffled_pages)(jax.random.split(jax.random.fold_in(key, 15), OWNERS)).astype(jnp.int32)
    slots = jnp.arange(MAXPAGES, dtype=jnp.int32)
    table_first = orders[:, slots % POOL]
    table_second = jnp.take_along_axis(orders, (first_pages[:, None] + slots[None, :]) % POOL, axis=1)
    tables = jnp.stack([table_first, table_second], axis=1).reshape(OWNERS * 2, MAXPAGES)
    held = jnp.stack([first, second], axis=1).reshape(OWNERS * 2)
    return (tables.astype(jnp.int32), held.astype(jnp.int32))


def draw_held_table(key, part):
    return pool_plan(key)[0]


def draw_held_len(key, part):
    return pool_plan(key)[1]


def draw_prev_owner(key, part):
    half_way = OWNERS // 2
    values = jnp.arange(OWNERS, dtype=jnp.int32)
    shuffled = jax.random.permutation(jax.random.fold_in(key, 21), OWNERS).astype(jnp.int32)
    shuffled_place = jnp.argsort(shuffled).astype(jnp.int32)
    fixed_rank = jnp.where(values == 0, 0, jnp.where(values == 1, 1, jnp.where(values == 1 + half_way, 2, jnp.where(values == half_way, 3, -1))))
    score = jnp.where(fixed_rank >= 0, fixed_rank, 4 + shuffled_place)
    order = jnp.argsort(score).astype(jnp.int32)
    offset = jax.random.randint(jax.random.fold_in(key, 22), (), 0, OWNERS)
    order = ((order + offset) % OWNERS).astype(jnp.int32)
    place = jnp.argsort(order)
    return order[(place + 1) % OWNERS].astype(jnp.int32)


def block_levels(key, shape, shards, smallest, largest):
    factor_of, own = 1.0, jax.random.fold_in(key, 6)
    for position, blocks in shards:
        heights = jnp.exp(jax.random.uniform(jax.random.fold_in(own, position), (blocks,), jnp.float32, smallest / len(shards), largest / len(shards)))
        factor_of = factor_of * jnp.repeat(heights, shape[position] // blocks).reshape([-1 if axis == position else 1 for axis in range(len(shape))])
    return factor_of


def centred(stream_key, shape, spread, bound, pieces=(), kind=jnp.bfloat16):
    entries = jax.random.normal(stream_key, shape, jnp.float32) * spread
    if len(pieces) > 0:
        entries = block_levels(stream_key, shape, pieces, -0.22, 0.18) * entries
    return jnp.clip(entries, min=-bound, max=bound).astype(kind)


def setup_inputs(seed: int = 0) -> dict:
    streams_of = jax.random.split(jax.random.key(seed), 17)
    return {
        "resid": draw_resid(jax.random.fold_in(streams_of[16], 71), 0),
        "q_in": draw_q_in(jax.random.fold_in(streams_of[16], 71), 0),
        "kv_in": draw_kv_in(jax.random.fold_in(streams_of[16], 71), 0),
        "parents": draw_parents(jax.random.fold_in(streams_of[16], 71), 0),
        "counts": draw_counts(jax.random.fold_in(streams_of[16], 71), 0),
        "accept_leaf": draw_accept_leaf(jax.random.fold_in(streams_of[16], 71), 0),
        "cache": centred(streams_of[6], (OWNERS * POOL, 2, PAGE, KV_HEADS * HEAD_DIM), 1.0, 6.0, ((0, 16), (3, 2))),
        "held_table": draw_held_table(jax.random.fold_in(streams_of[16], 71), 0),
        "held_len": draw_held_len(jax.random.fold_in(streams_of[16], 71), 0),
        "prev_owner": draw_prev_owner(jax.random.fold_in(streams_of[16], 71), 0),
        "w_out": centred(streams_of[10], (HEADS * HEAD_DIM, D), (HEADS * HEAD_DIM) ** -0.5, 0.125, ((0, 2),)),
        "gain_mid": jnp.clip(1.0 + 0.18 * jax.random.normal(streams_of[11], (D,), jnp.float32), 0.099609375, 1.8984375).astype(jnp.bfloat16),
        "w_in": centred(streams_of[12], (2, FF, D), D ** -0.5, 0.125, ((1, 32),)),
        "w_down": centred(streams_of[13], (FF, D), FF ** -0.5, 0.0625, ((0, 32),)),
        "gain_next": jnp.clip(1.0 + 0.18 * jax.random.normal(streams_of[14], (D,), jnp.float32), 0.099609375, 1.8984375).astype(jnp.bfloat16),
        "w_next": centred(streams_of[15], (D, QKV_WIDTH), D ** -0.5, 0.125, ((1, 2),)),
    }


norm_eps = 1e-05
masked_score = -1e+30

def ancestors(parents):
    count_nodes = parents.shape[-1]
    nodes = jnp.arange(count_nodes, dtype=jnp.int32)
    reach = (parents[..., :, None] == nodes).astype(jnp.float32) + jnp.eye(count_nodes, dtype=jnp.float32)
    for step in range(count_nodes.bit_length()):
        reach = jnp.minimum(jnp.einsum('sij,sjk->sik', reach, reach, precision=lax.Precision.HIGHEST), 1.0)
    return reach

def rms_scale(rows, gain):
    values = rows.astype(jnp.float32)
    factor = lax.rsqrt(lax.optimization_barrier(jnp.mean(values * values, axis=-1, keepdims=True)) + norm_eps)
    return (values * factor * gain.astype(jnp.float32)).astype(jnp.bfloat16)

def swiglu_rows(rows, w_in, w_down):
    dims = (((1,), (1,)), ((), ()))
    gate = lax.dot_general(rows, w_in[0], dims, preferred_element_type=jnp.float32)
    up_part = lax.dot_general(rows, w_in[1], dims, preferred_element_type=jnp.float32)
    hidden = (jax.nn.silu(gate) * up_part).astype(jnp.bfloat16)
    return jnp.dot(hidden, w_down, preferred_element_type=jnp.float32)

def compact_path(reach, leaves, rows):
    count_nodes = reach.shape[-1]
    nodes = jnp.arange(count_nodes, dtype=jnp.int32)
    leaf_hot = (nodes[None, :] == leaves[:, None]).astype(jnp.float32)
    path = jnp.einsum('si,sij->sj', leaf_hot, reach, precision=lax.Precision.HIGHEST)
    ranks = jnp.cumsum(path, axis=1) - path
    places = nodes.astype(jnp.float32)
    select = path[:, None, :] * (ranks[:, None, :] == places[None, :, None]).astype(jnp.float32)
    return jnp.einsum('spj,sjw->spw', select.astype(jnp.bfloat16), rows, preferred_element_type=jnp.float32).astype(jnp.bfloat16)

def request_attention(request, q_in, kv_in, reach, counts, cache, held_table, held_len, prev_owner):
    owner_dev = request // 2
    second = request % 2
    holder = jnp.where(second == 0, owner_dev, prev_owner[owner_dev]).astype(jnp.int32)
    row_id = (holder * 2 + second).astype(jnp.int32)
    page_ids = held_table[row_id] + holder * POOL
    held = cache[page_ids]
    key_rows = held[:, 0].reshape(MAXPAGES * PAGE, KV_HEADS, HEAD_DIM).astype(jnp.float32)
    value_rows = held[:, 1].reshape(MAXPAGES * PAGE, KV_HEADS, HEAD_DIM).astype(jnp.float32)
    first_row = (request * DRAFT).astype(jnp.int32)
    queries = lax.dynamic_slice_in_dim(q_in, first_row, DRAFT, 0).astype(jnp.float32).reshape(DRAFT, KV_HEADS, GROUP, HEAD_DIM)
    own_rows = lax.dynamic_slice_in_dim(kv_in, first_row, DRAFT, 0).astype(jnp.float32)
    draft_keys = own_rows[:, 0].reshape(DRAFT, KV_HEADS, HEAD_DIM)
    draft_values = own_rows[:, 1].reshape(DRAFT, KV_HEADS, HEAD_DIM)
    tree = lax.dynamic_index_in_dim(reach, request, 0, keepdims=False)
    count = lax.dynamic_index_in_dim(counts, request, 0, keepdims=False)
    allowed = (tree > 0.5) & (jnp.arange(DRAFT, dtype=jnp.int32)[None, :] < count)
    cached = jnp.arange(MAXPAGES * PAGE, dtype=jnp.int32) < held_len[row_id]
    scale = HEAD_DIM ** (-0.5)
    cache_scores = jnp.einsum('qghe,kge->ghqk', queries, key_rows) * scale
    cache_scores = jnp.where(cached, cache_scores, masked_score)
    tree_scores = jnp.einsum('qghe,kge->ghqk', queries, draft_keys) * scale
    tree_scores = jnp.where(allowed, tree_scores, masked_score)
    highest = jnp.maximum(lax.optimization_barrier(jnp.max(cache_scores, axis=-1)), lax.optimization_barrier(jnp.max(tree_scores, axis=-1)))
    cache_weights = jnp.where(cached, jnp.exp(cache_scores - highest[..., None]), 0.0)
    tree_weights = jnp.where(allowed, jnp.exp(tree_scores - highest[..., None]), 0.0)
    total = lax.optimization_barrier(jnp.sum(cache_weights, axis=-1)) + lax.optimization_barrier(jnp.sum(tree_weights, axis=-1))
    summed = jnp.einsum('ghqk,kge->ghqe', cache_weights, value_rows, precision=lax.Precision.HIGHEST)
    summed = summed + jnp.einsum('ghqk,kge->ghqe', tree_weights, draft_values, precision=lax.Precision.HIGHEST)
    result = summed / total[..., None]
    return jnp.transpose(result, (2, 0, 1, 3)).reshape(DRAFT, HEADS * HEAD_DIM).astype(jnp.bfloat16)

def reference(resid, q_in, kv_in, parents, counts, accept_leaf, cache, held_table, held_len, prev_owner, w_out, gain_mid, w_in, w_down, gain_next, w_next):
    reach = ancestors(parents)

    def one_request(request):
        return request_attention(request, q_in, kv_in, reach, counts, cache, held_table, held_len, prev_owner)
    attended = lax.map(one_request, jnp.arange(REQS, dtype=jnp.int32)).reshape(TOKENS, HEADS * HEAD_DIM)
    mixed = (resid.astype(jnp.float32) + jnp.dot(attended, w_out, preferred_element_type=jnp.float32)).astype(jnp.bfloat16)
    normed = rms_scale(mixed, gain_mid)
    hidden_out = (mixed.astype(jnp.float32) + swiglu_rows(normed, w_in, w_down)).astype(jnp.bfloat16)
    next_normed = rms_scale(hidden_out, gain_next)
    next_qkv = jnp.dot(next_normed, w_next, preferred_element_type=jnp.float32).astype(jnp.bfloat16)
    accepted = compact_path(reach, accept_leaf, kv_in.reshape(REQS, DRAFT, 2 * KV_HEADS * HEAD_DIM))
    accepted_kv = accepted.reshape(TOKENS, 2, KV_HEADS * HEAD_DIM)
    return (hidden_out, next_qkv, accepted_kv)
```

```python
import functools

import jax
import jax.numpy as jnp
from jax import lax
from jax.experimental import pallas as pl
from jax.experimental.pallas import tpu as pltpu
from jax.sharding import PartitionSpec as P

HEAD_DIM = 64
GROUP = 4
EPS = 1e-05
MESH = pl.DeviceIdType.MESH
F32 = jnp.float32
BF16 = jnp.bfloat16
VMEM = pltpu.VMEM
OWNER_LANE = 65
COUNT_LANE = 64


def layout(n):
    depth = 4 if n % 4 == 0 else 1
    return depth, n // depth


def position(n):
    depth, plane = layout(n)
    me = lax.axis_index("req")
    return me, me // plane, lax.rem(me, plane), lax.axis_index("mlp")


def greet(n, partner):
    depth, plane = layout(n)
    me, z, p, c = position(n)
    barrier = pltpu.get_barrier_semaphore()
    peers = [(lax.rem(z + k, depth) * plane + p, c) for k in range(1, depth)]
    peers += [(z * plane + lax.rem(p + k, plane), c) for k in range(1, plane)]
    if partner:
        peers.append((me, 1 - c))
    for peer in peers:
        pl.semaphore_signal(barrier, inc=1, device_id=peer, device_id_type=MESH)
    pl.semaphore_wait(barrier, len(peers))


def line_copies(n, ref, send_sem, recv_sem):
    depth, plane = layout(n)
    me, z, p, c = position(n)
    made = []
    for k in range(1, depth):
        made.append(
            pltpu.make_async_remote_copy(
                ref.at[me],
                ref.at[me],
                send_sem.at[k - 1],
                recv_sem.at[k - 1],
                device_id=(lax.rem(z + k, depth) * plane + p, c),
                device_id_type=MESH,
            )
        )
    return made


def plane_copies(n, ref, back, send_sem, recv_sem):
    depth, plane = layout(n)
    me, z, p, c = position(n)
    block = lax.rem(z - back + depth, depth) * plane + p
    made = []
    for k in range(1, plane):
        made.append(
            pltpu.make_async_remote_copy(
                ref.at[block],
                ref.at[block],
                send_sem.at[depth - 1 + back * (plane - 1) + k - 1],
                recv_sem.at[depth - 1 + back * (plane - 1) + k - 1],
                device_id=(z * plane + lax.rem(p + k, plane), c),
                device_id_type=MESH,
            )
        )
    return made


def parent_matrix(parents_ref, r):
    size = parents_ref.shape[1]
    row = lax.broadcasted_iota(jnp.int32, (size, 128), 0)
    lane = lax.broadcasted_iota(jnp.int32, (size, 128), 1)
    hot = jnp.zeros((size, 128), F32)
    for i in range(size):
        hot = jnp.where((row == i) & (lane == parents_ref[r, i]), 1.0, hot)
    return hot


def share_kernel(
    n, parents_ref, counts_ref, owner_ref, q_ref, kv_ref, resid_ref,
    out_ref, owners_ref, blocks, send_sem, recv_sem,
):
    depth, plane = layout(n)
    me, z, p, c = position(n)
    rows = out_ref.shape[0]
    qw, kw, half = q_ref.shape[1], kv_ref.shape[1], resid_ref.shape[1] // 2
    tail = qw + kw + half
    lane = lax.broadcasted_iota(jnp.int32, (rows, 128), 1)
    info = parent_matrix(parents_ref, 1)
    info = jnp.where(lane == COUNT_LANE, counts_ref[1].astype(F32), info)
    info = jnp.where(lane == OWNER_LANE, owner_ref[0].astype(F32), info)
    blocks[me, :, :qw] = q_ref[rows:, :]
    blocks[me, :, qw : qw + kw] = kv_ref[rows:, :]
    blocks[me, :, qw + kw : tail] = resid_ref[rows:, pl.ds(pl.multiple_of(c * half, 128), half)]
    blocks[me, :, tail:] = info.astype(BF16)
    greet(n, False)
    line = line_copies(n, blocks, send_sem, recv_sem)
    for copy in line:
        copy.start()
    started = list(line)
    for back in range(depth):
        if back:
            line[back - 1].wait_recv()
        made = plane_copies(n, blocks, back, send_sem, recv_sem)
        for copy in made:
            copy.start()
        started += made
    for copy in started[depth - 1 :]:
        copy.wait_recv()
    for copy in started:
        copy.wait_send()

    out_ref[...] = jnp.zeros_like(out_ref)

    def pick(j, carry):
        tags = blocks[j, :, tail:].astype(F32)
        owner = jnp.sum(jnp.where(lane == OWNER_LANE, tags, 0.0), axis=1, keepdims=True)
        owners_ref[j] = jnp.broadcast_to(owner, (rows, 128))[:8].astype(jnp.int32)
        mine = (owner == me.astype(F32)).astype(F32)
        out_ref[...] = (out_ref[...].astype(F32) + blocks[j].astype(F32) * mine).astype(BF16)
        return carry

    lax.fori_loop(0, n, pick, 0)


def roll_lanes(x, shift):
    w = x.shape[1]
    shift %= w
    if shift == 0:
        return x
    return jnp.concatenate([x[:, w - shift :], x[:, : w - shift]], axis=1)


def reach_of(hot):
    size = hot.shape[0]
    row = lax.broadcasted_iota(jnp.int32, (size, size), 0)
    col = lax.broadcasted_iota(jnp.int32, (size, size), 1)
    reach = hot + (row == col).astype(F32)
    for _ in range(size.bit_length()):
        twice = jnp.dot(reach.astype(BF16), reach.astype(BF16), preferred_element_type=F32)
        reach = jnp.minimum(twice, 1.0)
    return reach


def attend_kernel(
    pb, parents_ref, counts_ref, leaf_ref, table_ref, len_ref, q_ref, kv_ref, resid_ref, far_ref,
    cache_ref, w_out_ref, proj_ref, accepted_ref, pages, w_out, query, acc, peak, total, sem, w_sem,
):
    size = parents_ref.shape[1]
    qw, kw, half = q_ref.shape[1], kv_ref.shape[1], resid_ref.shape[1] // 2
    width = kw // 2
    heads = width // HEAD_DIM
    tail = qw + kw + half
    page_len = cache_ref.shape[2]
    keys = pb * page_len
    c = lax.axis_index("mlp")
    blocks = [(len_ref[s] + keys - 1) // keys for s in range(2)]

    for s in range(2):

        def fetch(b, carry):
            for i in range(pb):
                pltpu.make_async_copy(
                    cache_ref.at[table_ref[s, b * pb + i]], pages.at[s, b, i], sem.at[s, b]
                ).start()
            return carry

        lax.fori_loop(0, blocks[s], fetch, 0)
    w_copy = pltpu.make_async_copy(w_out_ref, w_out, w_sem)
    w_copy.start()

    row = lax.broadcasted_iota(jnp.int32, (size, size), 0)
    col = lax.broadcasted_iota(jnp.int32, (size, size), 1)
    lane = lax.broadcasted_iota(jnp.int32, (size, width), 1)
    tags = far_ref[:, tail:].astype(F32)
    near = [parent_matrix(parents_ref, s)[:, :size] for s in range(2)]
    far_hot = tags[:, :size]
    far_count = tags[:, COUNT_LANE : COUNT_LANE + 1]
    own_reach = [reach_of(hot) for hot in near]
    far_reach = reach_of(far_hot)

    before = (row < col).astype(BF16)
    for s in range(2):
        path = jnp.sum(jnp.where(row == leaf_ref[s], own_reach[s], 0.0), axis=0, keepdims=True)
        wide = jnp.broadcast_to(path, (size, size))
        ranks = jnp.dot(wide.astype(BF16), before, preferred_element_type=F32)
        select = jnp.where(ranks == row.astype(F32), wide, 0.0).astype(BF16)
        accepted_ref[s * size : (s + 1) * size, :] = jnp.dot(
            select, kv_ref[s * size : (s + 1) * size, :], preferred_element_type=F32
        ).astype(BF16)

    live = [
        jnp.where(col < counts_ref[0], own_reach[0], 0.0),
        jnp.where(col.astype(F32) < far_count, far_reach, 0.0),
    ]
    copies = GROUP * heads
    dims = (((1,), (1,)), ((), ()))
    for s in range(2):
        q_rows = (q_ref[:size, :] if s == 0 else far_ref[:, :qw]).astype(F32) * HEAD_DIM**-0.5
        parts = []
        for g in range(GROUP):
            for h in range(heads):
                piece = roll_lanes(q_rows[:, h * width : (h + 1) * width], (h - g) * HEAD_DIM)
                inside = (lane >= h * HEAD_DIM) & (lane < (h + 1) * HEAD_DIM)
                parts.append(jnp.where(inside, piece, 0.0))
        query[s] = jnp.concatenate(parts, axis=0).astype(BF16)
        draft = kv_ref[:size, :] if s == 0 else far_ref[:, qw : qw + kw]
        scores = lax.dot_general(query[s], draft[:, :width], dims, preferred_element_type=F32)
        open_ = jnp.concatenate([live[s]] * copies, axis=0) > 0.5
        scores = jnp.where(open_, scores, -1e30)
        top = jnp.max(scores, axis=1, keepdims=True)
        weights = jnp.where(open_, jnp.exp(scores - top), 0.0)
        peak[s] = jnp.broadcast_to(top, peak.shape[1:])
        total[s] = jnp.broadcast_to(jnp.sum(weights, axis=1, keepdims=True), total.shape[1:])
        acc[s] = jnp.dot(weights.astype(BF16), draft[:, width:], preferred_element_type=F32)

    for s in range(2):

        def step(b, carry):
            pltpu.make_async_copy(cache_ref.at[pl.ds(0, pb)], pages.at[s, b], sem.at[s, b]).wait()
            k = pages[s, b, :, 0].reshape(keys, width)
            v = pages[s, b, :, 1].reshape(keys, width)
            scores = lax.dot_general(query[s], k, dims, preferred_element_type=F32)
            places = b * keys + lax.broadcasted_iota(jnp.int32, scores.shape, 1)
            scores = jnp.where(places < len_ref[s], scores, -1e30)
            old = peak[s][:, :1]
            new = jnp.maximum(old, jnp.max(scores, axis=1, keepdims=True))
            weights = jnp.exp(scores - new)
            factor = jnp.exp(old - new)
            peak[s] = jnp.broadcast_to(new, peak.shape[1:])
            total[s] = total[s] * factor + jnp.sum(weights, axis=1, keepdims=True)
            acc[s] = acc[s] * factor + jnp.dot(weights.astype(BF16), v, preferred_element_type=F32)
            return carry

        lax.fori_loop(0, blocks[s], step, 0)

    done = []
    for s in range(2):
        result = acc[s] / total[s][:, :1]
        cols = []
        for h in range(heads):
            col_sum = jnp.zeros((size, width), F32)
            for g in range(GROUP):
                at = (g * heads + h) * size
                inside = (lane >= h * HEAD_DIM) & (lane < (h + 1) * HEAD_DIM)
                piece = jnp.where(inside, result[at : at + size], 0.0)
                col_sum = col_sum + roll_lanes(piece, (g - h) * HEAD_DIM)
            cols.append(col_sum)
        done.append(jnp.concatenate(cols, axis=1))
    attended = jnp.concatenate(done, axis=0).astype(BF16)
    w_copy.wait()
    proj_ref[...] = jnp.dot(attended, w_out[...], preferred_element_type=F32)
    mine = pl.ds(pl.multiple_of(c * half, 128), half)
    proj_ref[:size, mine] += resid_ref[:size, mine].astype(F32)
    proj_ref[size:, mine] += far_ref[:, qw + kw : tail].astype(F32)


def rms(values, gain):
    factor = lax.rsqrt(jnp.mean(values * values, axis=-1, keepdims=True) + EPS)
    return (values * factor * gain.astype(F32)).astype(BF16)


def layer_kernel(
    n, owners_ref, proj_ref, gain_mid_ref, gain_next_ref, w_in_hbm, w_down_hbm, w_next_hbm,
    hidden_ref, qkv_ref,
    w_in, w_down, w_next, other, mixed, rows_all, part, pair, ready, plane_in, line_out, line_in, final,
    w_sem, swap_sem, send_sem, recv_sem, fwd_send, fwd_recv, pair_send, pair_recv, rs_send, rs_recv,
):
    depth, plane = layout(n)
    me, z, p, c = position(n)
    size = ready.shape[1]
    width = ready.shape[2]
    loads = [
        pltpu.make_async_copy(src, dst, w_sem.at[i])
        for i, (src, dst) in enumerate(((w_in_hbm, w_in), (w_down_hbm, w_down), (w_next_hbm, w_next)))
    ]
    for load in loads:
        load.start()
    greet(n, True)
    partner = (me, 1 - c)
    swap = pltpu.make_async_remote_copy(
        proj_ref, other, swap_sem.at[0], swap_sem.at[1], device_id=partner, device_id_type=MESH
    )
    swap.start()
    swap.wait()
    both = (proj_ref[...] + other[...]).astype(BF16)
    mixed[0] = both[:size]
    mixed[1] = both[size:]
    mine = rows_all.at[c]
    rows_all[c, me] = rms(mixed[c].astype(F32), gain_mid_ref[...])

    line = line_copies(n, mine, send_sem, recv_sem)
    for copy in line:
        copy.start()
    by_back = []
    for back in range(depth):
        if back:
            line[back - 1].wait_recv()
        made = plane_copies(n, mine, back, send_sem, recv_sem)
        for copy in made:
            copy.start()
        by_back.append(made)
    loads[0].wait()
    loads[1].wait()

    def forward(back):
        group = pl.ds(lax.rem(z - back + depth, depth) * plane, plane)
        return pltpu.make_async_remote_copy(
            rows_all.at[c, group], rows_all.at[c, group],
            fwd_send.at[back], fwd_recv.at[back], device_id=partner, device_id_type=MESH,
        )

    def give(back):
        group = pl.ds(lax.rem(z - back + depth, depth) * plane, plane)
        return pltpu.make_async_remote_copy(
            part.at[1 - c, group], pair.at[group],
            pair_send.at[back], pair_recv.at[back], device_id=partner, device_id_type=MESH,
        )

    dims = (((1,), (1,)), ((), ()))
    for back in range(depth):
        for copy in by_back[back]:
            copy.wait_recv()
        forward(back).start()

    def feed(back, carry):
        forward(back).wait_recv()
        group = pl.ds(lax.rem(z - back + depth, depth) * plane, plane)
        x = rows_all[:, group].reshape(2 * plane * size, width)
        gate = lax.dot_general(x, w_in[0], dims, preferred_element_type=F32)
        up = lax.dot_general(x, w_in[1], dims, preferred_element_type=F32)
        hidden = (gate / (1.0 + jnp.exp(-gate)) * up).astype(BF16)
        y = jnp.dot(hidden, w_down[...], preferred_element_type=F32)
        part[:, group] = y.astype(BF16).reshape(2, plane, size, width)
        give(back).start()
        return carry

    lax.fori_loop(0, depth, feed, 0)
    part[c, me] = (part[c, me].astype(F32) + mixed[c].astype(F32)).astype(BF16)
    for back in range(depth):
        give(back).wait_recv()

    def gather_row(e, carry):
        d = e + c * (owners_ref[e] - e)
        ready[e] = (part[c, d].astype(F32) + pair[d].astype(F32)).astype(BF16)
        return carry

    lax.fori_loop(0, n, gather_row, 0)

    def to_plane(k, back):
        q = lax.rem(p + k, plane)
        i = (k - 1) * depth + back
        return pltpu.make_async_remote_copy(
            ready.at[lax.rem(z - back + depth, depth) * plane + q],
            plane_in.at[i],
            rs_send.at[i], rs_recv.at[i],
            device_id=(z * plane + q, c), device_id_type=MESH,
        )

    def to_line(back):
        i = (plane - 1) * depth + back
        return pltpu.make_async_remote_copy(
            line_out.at[back], line_in.at[back], rs_send.at[i], rs_recv.at[i],
            device_id=(lax.rem(z - back + depth, depth) * plane + p, c), device_id_type=MESH,
        )

    order = list(range(1, depth)) + [0]
    for back in order:
        for k in range(1, plane):
            to_plane(k, back).start()
    for back in order:
        for k in range(1, plane):
            to_plane(k, back).wait_recv()
        value = ready[lax.rem(z - back + depth, depth) * plane + p].astype(F32)
        for k in range(1, plane):
            value = value + plane_in[(k - 1) * depth + back].astype(F32)
        if back:
            line_out[back] = value.astype(BF16)
            to_line(back).start()
    for back in range(1, depth):
        to_line(back).wait_recv()
        value = value + line_in[back].astype(F32)
    final[c] = value.astype(BF16)
    last = pltpu.make_async_remote_copy(
        final.at[c], final.at[c], swap_sem.at[2], swap_sem.at[3], device_id=partner, device_id_type=MESH
    )
    last.start()
    loads[2].wait()
    last.wait()
    rows = jnp.concatenate([final[0], final[1]], axis=0)
    hidden_ref[...] = rows
    qkv_ref[...] = jnp.dot(
        rms(rows.astype(F32), gain_next_ref[...]), w_next[...], preferred_element_type=F32
    ).astype(BF16)
    for copy in line:
        copy.wait_send()
    for back in range(depth):
        for copy in by_back[back]:
            copy.wait_send()
        forward(back).wait_send()
        give(back).wait_send()
        for k in range(1, plane):
            to_plane(k, back).wait_send()
        if back:
            to_line(back).wait_send()


def per_device(
    n, resid, q_in, kv_in, parents, counts, accept_leaf, cache, held_table, held_len, prev_owner,
    w_out, gain_mid, w_in, w_down, gain_next, w_next,
):
    depth, plane = layout(n)
    size = parents.shape[1]
    width = resid.shape[1]
    qw = q_in.shape[1]
    kw = 2 * kv_in.shape[2]
    kv = kv_in.reshape(2 * size, kw)
    block = qw + kw + width // 2 + 128
    smem = pl.BlockSpec(memory_space=pltpu.SMEM)
    vmem = pl.BlockSpec(memory_space=VMEM)
    hbm = pl.BlockSpec(memory_space=pl.ANY)
    dma = pltpu.SemaphoreType.DMA
    sends = depth - 1 + depth * (plane - 1)
    far, owners = pl.pallas_call(
        functools.partial(share_kernel, n),
        out_shape=(
            jax.ShapeDtypeStruct((size, block), BF16),
            jax.ShapeDtypeStruct((n, 8, 128), jnp.int32),
        ),
        in_specs=[smem] * 3 + [vmem] * 3,
        out_specs=(vmem, vmem),
        scratch_shapes=[VMEM((n, size, block), BF16), dma((sends,)), dma((sends,))],
        compiler_params=pltpu.CompilerParams(
            collective_id=0, has_side_effects=True, vmem_limit_bytes=24 << 20
        ),
        name="share",
    )(parents, counts, prev_owner, q_in, kv, resid)

    pb = 4
    num_blocks = held_table.shape[1] // pb
    query_rows = size * qw // HEAD_DIM
    proj, accepted = pl.pallas_call(
        functools.partial(attend_kernel, pb),
        out_shape=(
            jax.ShapeDtypeStruct((2 * size, width), F32),
            jax.ShapeDtypeStruct((2 * size, kw), BF16),
        ),
        in_specs=[smem] * 5 + [vmem] * 4 + [hbm] * 2,
        out_specs=(vmem, vmem),
        scratch_shapes=[
            VMEM((2, num_blocks, pb) + cache.shape[1:], BF16),
            VMEM(w_out.shape, BF16),
            VMEM((2, query_rows, kw // 2), BF16),
            VMEM((2, query_rows, kw // 2), F32),
            VMEM((2, query_rows, 128), F32),
            VMEM((2, query_rows, 128), F32),
            dma((2, num_blocks)),
            dma,
        ],
        compiler_params=pltpu.CompilerParams(vmem_limit_bytes=48 << 20),
        name="attend",
    )(parents, counts, accept_leaf, held_table, held_len, q_in, kv, resid, far, cache, w_out)

    rows = (size, width)
    hidden_out, next_qkv = pl.pallas_call(
        functools.partial(layer_kernel, n),
        out_shape=(
            jax.ShapeDtypeStruct((2 * size, width), BF16),
            jax.ShapeDtypeStruct((2 * size, w_next.shape[1]), BF16),
        ),
        in_specs=[smem] + [vmem] * 3 + [hbm] * 3,
        out_specs=(vmem, vmem),
        scratch_shapes=[
            VMEM(w_in.shape, BF16),
            VMEM(w_down.shape, BF16),
            VMEM(w_next.shape, BF16),
            VMEM((2 * size, width), F32),
            VMEM((2,) + rows, BF16),
            VMEM((2, n) + rows, BF16),
            VMEM((2, n) + rows, BF16),
            VMEM((n,) + rows, BF16),
            VMEM((n,) + rows, BF16),
            VMEM(((plane - 1) * depth,) + rows, BF16),
            VMEM((depth,) + rows, BF16),
            VMEM((depth,) + rows, BF16),
            VMEM((2,) + rows, BF16),
            dma((3,)),
            dma((4,)),
            dma((sends,)),
            dma((sends,)),
            dma((depth,)),
            dma((depth,)),
            dma((depth,)),
            dma((depth,)),
            dma((plane * depth,)),
            dma((plane * depth,)),
        ],
        compiler_params=pltpu.CompilerParams(
            collective_id=1, has_side_effects=True, vmem_limit_bytes=60 << 20
        ),
        name="layer",
    )(
        owners[:, 0, 0], proj, gain_mid.reshape(1, width), gain_next.reshape(1, width),
        w_in, w_down, w_next,
    )
    return hidden_out, next_qkv, accepted.reshape(kv_in.shape)


def solution(mesh):
    placed = (
        P("req", None),
        P("req", "mlp"),
        P("req", None, "mlp"),
        P("req", None),
        P("req"),
        P("req"),
        P("req", None, None, "mlp"),
        P("req", None),
        P("req"),
        P("req"),
        P("mlp", None),
        P(),
        P(None, ("req", "mlp"), None),
        P(("req", "mlp"), None),
        P(),
        P(None, "mlp"),
    )
    return jax.shard_map(
        functools.partial(per_device, mesh.shape["req"]),
        mesh=mesh,
        in_specs=placed,
        out_specs=(P("req", None), P("req", "mlp"), P("req", None, "mlp")),
        check_vma=False,
    )
```

```python
import functools

import jax
import jax.numpy as jnp
from jax import lax
from jax.experimental import pallas as pl
from jax.experimental.pallas import tpu as pltpu
from jax.sharding import PartitionSpec as P

HEAD_DIM = 64
GROUP = 4
EPS = 1e-05
MESH = pl.DeviceIdType.MESH
F32 = jnp.float32
BF16 = jnp.bfloat16
VMEM = pltpu.VMEM
OWNER_LANE = 65
COUNT_LANE = 64


def layout(n):
    depth = 4 if n % 4 == 0 else 1
    return depth, n // depth


def position(n):
    depth, plane = layout(n)
    me = lax.axis_index("req")
    return me, me // plane, lax.rem(me, plane), lax.axis_index("mlp")


def greet(n, partner):
    depth, plane = layout(n)
    me, z, p, c = position(n)
    barrier = pltpu.get_barrier_semaphore()
    peers = [(lax.rem(z + k, depth) * plane + p, c) for k in range(1, depth)]
    peers += [(z * plane + lax.rem(p + k, plane), c) for k in range(1, plane)]
    if partner:
        peers.append((me, 1 - c))
    for peer in peers:
        pl.semaphore_signal(barrier, inc=1, device_id=peer, device_id_type=MESH)
    pl.semaphore_wait(barrier, len(peers))


def line_copies(n, ref, send_sem, recv_sem):
    depth, plane = layout(n)
    me, z, p, c = position(n)
    made = []
    for k in range(1, depth):
        made.append(
            pltpu.make_async_remote_copy(
                ref.at[me],
                ref.at[me],
                send_sem.at[k - 1],
                recv_sem.at[k - 1],
                device_id=(lax.rem(z + k, depth) * plane + p, c),
                device_id_type=MESH,
            )
        )
    return made


def plane_copies(n, ref, back, send_sem, recv_sem):
    depth, plane = layout(n)
    me, z, p, c = position(n)
    base = lax.rem(z - back + depth, depth) * plane

    def copy(view, place, i):
        at = depth - 1 + back * plane + i
        return pltpu.make_async_remote_copy(
            view, view, send_sem.at[at], recv_sem.at[at],
            device_id=(z * plane + place, c), device_id_type=MESH,
        )

    if plane != 4:
        return [copy(ref.at[base + p], lax.rem(p + k, plane), k - 1) for k in range(1, plane)], []
    width = ref.shape[-1]
    cut = width // 256 * 128
    side, across = p + 1 - 2 * lax.rem(p, 2), lax.rem(p + 2, 4)
    first = [copy(ref.at[base + p], side, 0), copy(ref.at[base + p], across, 1)]
    relays = [
        copy(ref.at[base + side, :, pl.ds(0, cut)], across, 2),
        copy(ref.at[base + across, :, pl.ds(cut, width - cut)], side, 3),
    ]
    return first, relays


def run_plane(made, started):
    first, relays = made
    for i, relay in enumerate(relays):
        first[i].wait_recv()
        relay.start()
    started += first + relays
    for copy in relays if relays else first:
        copy.wait_recv()


def parent_matrix(parents_ref, r):
    size = parents_ref.shape[1]
    row = lax.broadcasted_iota(jnp.int32, (size, 128), 0)
    lane = lax.broadcasted_iota(jnp.int32, (size, 128), 1)
    hot = jnp.zeros((size, 128), F32)
    for i in range(size):
        hot = jnp.where((row == i) & (lane == parents_ref[r, i]), 1.0, hot)
    return hot


def fetch_all(sem, *pairs):
    loads = [pltpu.make_async_copy(src, dst, sem.at[i]) for i, (src, dst) in enumerate(pairs)]
    for load in loads:
        load.start()
    return loads


def share_kernel(
    n, parents_ref, counts_ref, owner_ref, q_ref, kv_ref, resid_ref,
    out_ref, owners_ref, blocks, send_sem, recv_sem, parents_s, counts_s, owner_s, load_sem,
):
    depth, plane = layout(n)
    me, z, p, c = position(n)
    rows = out_ref.shape[0]
    qw, kw, half = q_ref.shape[1], kv_ref.shape[1], resid_ref.shape[1] // 2
    tail = qw + kw + half
    lane = lax.broadcasted_iota(jnp.int32, (rows, 128), 1)
    second = pl.ds(rows, rows)
    own_half = pl.ds(pl.multiple_of(c * half, 128), half)
    loads = fetch_all(
        load_sem,
        (parents_ref, parents_s),
        (counts_ref, counts_s),
        (owner_ref, owner_s),
        (q_ref.at[second], blocks.at[me, :, pl.ds(0, qw)]),
        (kv_ref.at[second], blocks.at[me, :, pl.ds(qw, kw)]),
        (resid_ref.at[second, own_half], blocks.at[me, :, pl.ds(qw + kw, half)]),
    )
    greet(n, False)
    for load in loads:
        load.wait()
    info = parent_matrix(parents_s, 1)
    info = jnp.where(lane == COUNT_LANE, counts_s[1].astype(F32), info)
    info = jnp.where(lane == OWNER_LANE, owner_s[0].astype(F32), info)
    blocks[me, :, tail:] = info.astype(BF16)
    line = line_copies(n, blocks, send_sem, recv_sem)
    for copy in line:
        copy.start()
    started = list(line)
    waiting = None
    for back in range(depth):
        if back:
            line[back - 1].wait_recv()
        made = plane_copies(n, blocks, back, send_sem, recv_sem)
        for copy in made[0]:
            copy.start()
        if waiting:
            run_plane(waiting, started)
        waiting = made
    run_plane(waiting, started)
    for copy in started:
        copy.wait_send()

    out_ref[...] = jnp.zeros_like(out_ref)

    def pick(j, carry):
        tags = blocks[j, :, tail:].astype(F32)
        owner = jnp.sum(jnp.where(lane == OWNER_LANE, tags, 0.0), axis=1, keepdims=True)
        owners_ref[pl.ds(j, 1), :] = jnp.broadcast_to(owner, (rows, 128))[:1].astype(jnp.int32)
        mine = (owner == me.astype(F32)).astype(F32)
        out_ref[...] = (out_ref[...].astype(F32) + blocks[j].astype(F32) * mine).astype(BF16)
        return carry

    lax.fori_loop(0, n, pick, 0)


def roll_lanes(x, shift):
    w = x.shape[1]
    shift %= w
    if shift == 0:
        return x
    return jnp.concatenate([x[:, w - shift :], x[:, : w - shift]], axis=1)


def reach_of(hot):
    size = hot.shape[0]
    row = lax.broadcasted_iota(jnp.int32, (size, size), 0)
    col = lax.broadcasted_iota(jnp.int32, (size, size), 1)
    reach = hot + (row == col).astype(F32)
    for _ in range(size.bit_length()):
        twice = jnp.dot(reach.astype(BF16), reach.astype(BF16), preferred_element_type=F32)
        reach = jnp.minimum(twice, 1.0)
    return reach


def attend_kernel(
    pb, parents_ref, counts_ref, leaf_ref, table_ref, len_ref, q_ref, kv_ref, resid_ref, far_ref,
    cache_ref, w_out_ref, proj_ref, accepted_ref, pages, w_out, query, acc, peak, total, sem, w_sem,
    parents_s, counts_s, leaf_s, table_s, len_s, q_v, kv_v, resid_v, load_sem,
):
    loads = fetch_all(
        load_sem,
        (table_ref, table_s), (len_ref, len_s), (parents_ref, parents_s), (counts_ref, counts_s),
        (leaf_ref, leaf_s), (q_ref, q_v), (kv_ref, kv_v), (resid_ref, resid_v),
    )
    loads[0].wait()
    loads[1].wait()
    parents_ref, counts_ref, leaf_ref, table_ref, len_ref = parents_s, counts_s, leaf_s, table_s, len_s
    q_ref, kv_ref, resid_ref = q_v, kv_v, resid_v
    size = parents_ref.shape[1]
    qw, kw, half = q_ref.shape[1], kv_ref.shape[1], resid_ref.shape[1] // 2
    width = kw // 2
    heads = width // HEAD_DIM
    tail = qw + kw + half
    page_len = cache_ref.shape[2]
    keys = pb * page_len
    c = lax.axis_index("mlp")
    blocks = [(len_ref[s] + keys - 1) // keys for s in range(2)]

    for s in range(2):

        def fetch(b, carry):
            for i in range(pb):
                pltpu.make_async_copy(
                    cache_ref.at[table_ref[s, b * pb + i]], pages.at[s, b, i], sem.at[s, b]
                ).start()
            return carry

        lax.fori_loop(0, blocks[s], fetch, 0)
    w_copy = pltpu.make_async_copy(w_out_ref, w_out, w_sem)
    w_copy.start()
    for load in loads[2:]:
        load.wait()

    row = lax.broadcasted_iota(jnp.int32, (size, size), 0)
    col = lax.broadcasted_iota(jnp.int32, (size, size), 1)
    lane = lax.broadcasted_iota(jnp.int32, (size, width), 1)
    tags = far_ref[:, tail:].astype(F32)
    near = [parent_matrix(parents_ref, s)[:, :size] for s in range(2)]
    far_hot = tags[:, :size]
    far_count = tags[:, COUNT_LANE : COUNT_LANE + 1]
    own_reach = [reach_of(hot) for hot in near]
    far_reach = reach_of(far_hot)

    before = (row < col).astype(BF16)
    for s in range(2):
        path = jnp.sum(jnp.where(row == leaf_ref[s], own_reach[s], 0.0), axis=0, keepdims=True)
        wide = jnp.broadcast_to(path, (size, size))
        ranks = jnp.dot(wide.astype(BF16), before, preferred_element_type=F32)
        select = jnp.where(ranks == row.astype(F32), wide, 0.0).astype(BF16)
        accepted_ref[s * size : (s + 1) * size, :] = jnp.dot(
            select, kv_ref[s * size : (s + 1) * size, :], preferred_element_type=F32
        ).astype(BF16)

    live = [
        jnp.where(col < counts_ref[0], own_reach[0], 0.0),
        jnp.where(col.astype(F32) < far_count, far_reach, 0.0),
    ]
    copies = GROUP * heads
    dims = (((1,), (1,)), ((), ()))
    for s in range(2):
        q_rows = (q_ref[:size, :] if s == 0 else far_ref[:, :qw]).astype(F32) * HEAD_DIM**-0.5
        parts = []
        for g in range(GROUP):
            for h in range(heads):
                piece = roll_lanes(q_rows[:, h * width : (h + 1) * width], (h - g) * HEAD_DIM)
                inside = (lane >= h * HEAD_DIM) & (lane < (h + 1) * HEAD_DIM)
                parts.append(jnp.where(inside, piece, 0.0))
        query[s] = jnp.concatenate(parts, axis=0).astype(BF16)
        draft = kv_ref[:size, :] if s == 0 else far_ref[:, qw : qw + kw]
        scores = lax.dot_general(query[s], draft[:, :width], dims, preferred_element_type=F32)
        open_ = jnp.concatenate([live[s]] * copies, axis=0) > 0.5
        scores = jnp.where(open_, scores, -1e30)
        top = jnp.max(scores, axis=1, keepdims=True)
        weights = jnp.where(open_, jnp.exp(scores - top), 0.0)
        peak[s] = jnp.broadcast_to(top, peak.shape[1:])
        total[s] = jnp.broadcast_to(jnp.sum(weights, axis=1, keepdims=True), total.shape[1:])
        acc[s] = jnp.dot(weights.astype(BF16), draft[:, width:], preferred_element_type=F32)

    for s in range(2):

        def step(b, carry):
            pltpu.make_async_copy(cache_ref.at[pl.ds(0, pb)], pages.at[s, b], sem.at[s, b]).wait()
            k = pages[s, b, :, 0].reshape(keys, width)
            v = pages[s, b, :, 1].reshape(keys, width)
            scores = lax.dot_general(query[s], k, dims, preferred_element_type=F32)
            places = b * keys + lax.broadcasted_iota(jnp.int32, scores.shape, 1)
            scores = jnp.where(places < len_ref[s], scores, -1e30)
            old = peak[s][:, :1]
            new = jnp.maximum(old, jnp.max(scores, axis=1, keepdims=True))
            weights = jnp.exp(scores - new)
            factor = jnp.exp(old - new)
            peak[s] = jnp.broadcast_to(new, peak.shape[1:])
            total[s] = total[s] * factor + jnp.sum(weights, axis=1, keepdims=True)
            acc[s] = acc[s] * factor + jnp.dot(weights.astype(BF16), v, preferred_element_type=F32)
            return carry

        lax.fori_loop(0, blocks[s], step, 0)

    done = []
    for s in range(2):
        result = acc[s] / total[s][:, :1]
        cols = []
        for h in range(heads):
            col_sum = jnp.zeros((size, width), F32)
            for g in range(GROUP):
                at = (g * heads + h) * size
                inside = (lane >= h * HEAD_DIM) & (lane < (h + 1) * HEAD_DIM)
                piece = jnp.where(inside, result[at : at + size], 0.0)
                col_sum = col_sum + roll_lanes(piece, (g - h) * HEAD_DIM)
            cols.append(col_sum)
        done.append(jnp.concatenate(cols, axis=1))
    attended = jnp.concatenate(done, axis=0).astype(BF16)
    w_copy.wait()
    proj_ref[...] = jnp.dot(attended, w_out[...], preferred_element_type=F32)
    mine = pl.ds(pl.multiple_of(c * half, 128), half)
    proj_ref[:size, mine] += resid_ref[:size, mine].astype(F32)
    proj_ref[size:, mine] += far_ref[:, qw + kw : tail].astype(F32)


def rms(values, gain):
    factor = lax.rsqrt(jnp.mean(values * values, axis=-1, keepdims=True) + EPS)
    return (values * factor * gain.astype(F32).reshape(1, -1)).astype(BF16)


def layer_kernel(
    n, owners_ref, proj_ref, gain_mid_ref, gain_next_ref, w_in_hbm, w_down_hbm, w_next_hbm,
    hidden_ref, qkv_ref,
    w_in, w_down, w_next, other, mixed, rows_all, part, pair, ready, plane_in, line_out, line_in, final,
    w_sem, swap_sem, send_sem, recv_sem, fwd_send, fwd_recv, pair_send, pair_recv, rs_send, rs_recv,
):
    depth, plane = layout(n)
    me, z, p, c = position(n)
    size = ready.shape[1]
    width = ready.shape[2]
    loads = [
        pltpu.make_async_copy(src, dst, w_sem.at[i])
        for i, (src, dst) in enumerate(((w_in_hbm, w_in), (w_down_hbm, w_down), (w_next_hbm, w_next)))
    ]
    for load in loads:
        load.start()
    greet(n, True)
    partner = (me, 1 - c)
    swap = pltpu.make_async_remote_copy(
        proj_ref, other, swap_sem.at[0], swap_sem.at[1], device_id=partner, device_id_type=MESH
    )
    swap.start()
    swap.wait()
    both = (proj_ref[...] + other[...]).astype(BF16)
    mixed[0] = both[:size]
    mixed[1] = both[size:]
    mine = rows_all.at[c]
    rows_all[c, me] = rms(mixed[c].astype(F32), gain_mid_ref[...])

    line = line_copies(n, mine, send_sem, recv_sem)
    for copy in line:
        copy.start()
    def forward(back):
        group = pl.ds(lax.rem(z - back + depth, depth) * plane, plane)
        return pltpu.make_async_remote_copy(
            rows_all.at[c, group], rows_all.at[c, group],
            fwd_send.at[back], fwd_recv.at[back], device_id=partner, device_id_type=MESH,
        )

    def give(back):
        group = pl.ds(lax.rem(z - back + depth, depth) * plane, plane)
        return pltpu.make_async_remote_copy(
            part.at[1 - c, group], pair.at[group],
            pair_send.at[back], pair_recv.at[back], device_id=partner, device_id_type=MESH,
        )

    dims = (((1,), (1,)), ((), ()))

    def feed(back):
        forward(back).wait_recv()
        group = pl.ds(lax.rem(z - back + depth, depth) * plane, plane)
        x = rows_all[:, group].reshape(2 * plane * size, width)
        gate = lax.dot_general(x, w_in[0], dims, preferred_element_type=F32)
        up = lax.dot_general(x, w_in[1], dims, preferred_element_type=F32)
        hidden = (gate / (1.0 + jnp.exp(-gate)) * up).astype(BF16)
        y = jnp.dot(hidden, w_down[...], preferred_element_type=F32)
        part[:, group] = y.astype(BF16).reshape(2, plane, size, width)
        give(back).start()

    started = list(line)
    made = plane_copies(n, mine, 0, send_sem, recv_sem)
    for copy in made[0]:
        copy.start()
    for back in range(depth):
        waiting = made
        if back + 1 < depth:
            line[back].wait_recv()
            made = plane_copies(n, mine, back + 1, send_sem, recv_sem)
            for copy in made[0]:
                copy.start()
        run_plane(waiting, started)
        forward(back).start()
        if back == 0:
            loads[0].wait()
            loads[1].wait()
        else:
            feed(back - 1)
    feed(depth - 1)
    part[c, me] = (part[c, me].astype(F32) + mixed[c].astype(F32)).astype(BF16)
    for back in range(depth):
        give(back).wait_recv()

    def gather_row(e, carry):
        d = e + c * (owners_ref[e, 0] - e)
        ready[e] = (part[c, d].astype(F32) + pair[d].astype(F32)).astype(BF16)
        return carry

    lax.fori_loop(0, n, gather_row, 0)

    def to_plane(k, back):
        q = lax.rem(p + k, plane)
        i = (k - 1) * depth + back
        return pltpu.make_async_remote_copy(
            ready.at[lax.rem(z - back + depth, depth) * plane + q],
            plane_in.at[i],
            rs_send.at[i], rs_recv.at[i],
            device_id=(z * plane + q, c), device_id_type=MESH,
        )

    def to_line(back):
        i = (plane - 1) * depth + back
        return pltpu.make_async_remote_copy(
            line_out.at[back], line_in.at[back], rs_send.at[i], rs_recv.at[i],
            device_id=(lax.rem(z - back + depth, depth) * plane + p, c), device_id_type=MESH,
        )

    order = list(range(1, depth)) + [0]
    for back in order:
        for k in range(1, plane):
            to_plane(k, back).start()
    for back in order:
        for k in range(1, plane):
            to_plane(k, back).wait_recv()
        value = ready[lax.rem(z - back + depth, depth) * plane + p].astype(F32)
        for k in range(1, plane):
            value = value + plane_in[(k - 1) * depth + back].astype(F32)
        if back:
            line_out[back] = value.astype(BF16)
            to_line(back).start()
    for back in range(1, depth):
        to_line(back).wait_recv()
        value = value + line_in[back].astype(F32)
    final[c] = value.astype(BF16)
    last = pltpu.make_async_remote_copy(
        final.at[c], final.at[c], swap_sem.at[2], swap_sem.at[3], device_id=partner, device_id_type=MESH
    )
    last.start()
    loads[2].wait()
    last.wait()
    rows = jnp.concatenate([final[0], final[1]], axis=0)
    hidden_ref[...] = rows
    qkv_ref[...] = jnp.dot(
        rms(rows.astype(F32), gain_next_ref[...]), w_next[...], preferred_element_type=F32
    ).astype(BF16)
    for copy in started:
        copy.wait_send()
    for back in range(depth):
        forward(back).wait_send()
        give(back).wait_send()
        for k in range(1, plane):
            to_plane(k, back).wait_send()
        if back:
            to_line(back).wait_send()


def per_device(
    n, resid, q_in, kv_in, parents, counts, accept_leaf, cache, held_table, held_len, prev_owner,
    w_out, gain_mid, w_in, w_down, gain_next, w_next,
):
    depth, plane = layout(n)
    size = parents.shape[1]
    width = resid.shape[1]
    qw = q_in.shape[1]
    kw = 2 * kv_in.shape[2]
    kv = kv_in.reshape(2 * size, kw)
    block = qw + kw + width // 2 + 128
    smem = pl.BlockSpec(memory_space=pltpu.SMEM)
    vmem = pl.BlockSpec(memory_space=VMEM)
    hbm = pl.BlockSpec(memory_space=pl.ANY)
    dma = pltpu.SemaphoreType.DMA

    def smem_of(array):
        return pltpu.SMEM(array.shape, array.dtype)

    sends = depth - 1 + depth * plane
    far, owners = pl.pallas_call(
        functools.partial(share_kernel, n),
        out_shape=(
            jax.ShapeDtypeStruct((size, block), BF16),
            jax.ShapeDtypeStruct((n, 128), jnp.int32),
        ),
        in_specs=[hbm] * 6,
        out_specs=(vmem, vmem),
        scratch_shapes=[
            VMEM((n, size, block), BF16), dma((sends,)), dma((sends,)),
            smem_of(parents), smem_of(counts), smem_of(prev_owner), dma((6,)),
        ],
        compiler_params=pltpu.CompilerParams(
            collective_id=0, has_side_effects=True, vmem_limit_bytes=60 << 20
        ),
        name="share",
    )(parents, counts, prev_owner, q_in, kv, resid)

    pb = 4
    num_blocks = held_table.shape[1] // pb
    query_rows = size * qw // HEAD_DIM
    proj, accepted = pl.pallas_call(
        functools.partial(attend_kernel, pb),
        out_shape=(
            jax.ShapeDtypeStruct((2 * size, width), F32),
            jax.ShapeDtypeStruct((2 * size, kw), BF16),
        ),
        in_specs=[hbm] * 8 + [vmem] + [hbm] * 2,
        out_specs=(vmem, vmem),
        scratch_shapes=[
            VMEM((2, num_blocks, pb) + cache.shape[1:], BF16),
            VMEM(w_out.shape, BF16),
            VMEM((2, query_rows, kw // 2), BF16),
            VMEM((2, query_rows, kw // 2), F32),
            VMEM((2, query_rows, 128), F32),
            VMEM((2, query_rows, 128), F32),
            dma((2, num_blocks)),
            dma,
            smem_of(parents), smem_of(counts), smem_of(accept_leaf), smem_of(held_table), smem_of(held_len),
            VMEM(q_in.shape, BF16), VMEM(kv.shape, BF16), VMEM(resid.shape, BF16), dma((8,)),
        ],
        compiler_params=pltpu.CompilerParams(vmem_limit_bytes=60 << 20),
        name="attend",
    )(parents, counts, accept_leaf, held_table, held_len, q_in, kv, resid, far, cache, w_out)

    rows = (size, width)
    hidden_out, next_qkv = pl.pallas_call(
        functools.partial(layer_kernel, n),
        out_shape=(
            jax.ShapeDtypeStruct((2 * size, width), BF16),
            jax.ShapeDtypeStruct((2 * size, w_next.shape[1]), BF16),
        ),
        in_specs=[smem] + [vmem] * 3 + [hbm] * 3,
        out_specs=(vmem, vmem),
        scratch_shapes=[
            VMEM(w_in.shape, BF16),
            VMEM(w_down.shape, BF16),
            VMEM(w_next.shape, BF16),
            VMEM((2 * size, width), F32),
            VMEM((2,) + rows, BF16),
            VMEM((2, n) + rows, BF16),
            VMEM((2, n) + rows, BF16),
            VMEM((n,) + rows, BF16),
            VMEM((n,) + rows, BF16),
            VMEM(((plane - 1) * depth,) + rows, BF16),
            VMEM((depth,) + rows, BF16),
            VMEM((depth,) + rows, BF16),
            VMEM((2,) + rows, BF16),
            dma((3,)),
            dma((4,)),
            dma((sends,)),
            dma((sends,)),
            dma((depth,)),
            dma((depth,)),
            dma((depth,)),
            dma((depth,)),
            dma((plane * depth,)),
            dma((plane * depth,)),
        ],
        compiler_params=pltpu.CompilerParams(
            collective_id=1, has_side_effects=True, vmem_limit_bytes=60 << 20
        ),
        name="layer",
    )(
        owners, proj, gain_mid, gain_next,
        w_in, w_down, w_next,
    )
    return hidden_out, next_qkv, accepted.reshape(kv_in.shape)


def solution(mesh):
    placed = (
        P("req", None),
        P("req", "mlp"),
        P("req", None, "mlp"),
        P("req", None),
        P("req"),
        P("req"),
        P("req", None, None, "mlp"),
        P("req", None),
        P("req"),
        P("req"),
        P("mlp", None),
        P(),
        P(None, ("req", "mlp"), None),
        P(("req", "mlp"), None),
        P(),
        P(None, "mlp"),
    )
    return jax.shard_map(
        functools.partial(per_device, mesh.shape["req"]),
        mesh=mesh,
        in_specs=placed,
        out_specs=(P("req", None), P("req", "mlp"), P("req", None, "mlp")),
        check_vma=False,
    )
```

```python
import functools

import jax
import jax.numpy as jnp
from jax import lax
from jax.experimental import pallas as pl
from jax.experimental.pallas import tpu as pltpu
from jax.sharding import PartitionSpec as P

HEAD_DIM = 64
GROUP = 4
EPS = 1e-05
MESH = pl.DeviceIdType.MESH
F32 = jnp.float32
BF16 = jnp.bfloat16
VMEM = pltpu.VMEM
OWNER_LANE = 65
COUNT_LANE = 64


def layout(n):
    depth = 4 if n % 4 == 0 else 1
    return depth, n // depth


def position(n):
    depth, plane = layout(n)
    me = lax.axis_index("req")
    return me, me // plane, lax.rem(me, plane), lax.axis_index("mlp")


def greet(n, partner):
    depth, plane = layout(n)
    me, z, p, c = position(n)
    barrier = pltpu.get_barrier_semaphore()
    peers = [(lax.rem(z + k, depth) * plane + p, c) for k in range(1, depth)]
    peers += [(z * plane + lax.rem(p + k, plane), c) for k in range(1, plane)]
    if partner:
        peers.append((me, 1 - c))
    for peer in peers:
        pl.semaphore_signal(barrier, inc=1, device_id=peer, device_id_type=MESH)
    pl.semaphore_wait(barrier, len(peers))


def line_copies(n, ref, send_sem, recv_sem):
    depth, plane = layout(n)
    me, z, p, c = position(n)
    made = []
    for k in range(1, depth):
        made.append(
            pltpu.make_async_remote_copy(
                ref.at[me],
                ref.at[me],
                send_sem.at[k - 1],
                recv_sem.at[k - 1],
                device_id=(lax.rem(z + k, depth) * plane + p, c),
                device_id_type=MESH,
            )
        )
    return made


def plane_copies(n, ref, back, send_sem, recv_sem):
    depth, plane = layout(n)
    me, z, p, c = position(n)
    base = lax.rem(z - back + depth, depth) * plane

    def copy(view, place, i):
        at = depth - 1 + back * plane + i
        return pltpu.make_async_remote_copy(
            view, view, send_sem.at[at], recv_sem.at[at],
            device_id=(z * plane + place, c), device_id_type=MESH,
        )

    return [copy(ref.at[base + p], lax.rem(p + k, plane), k - 1) for k in range(1, plane)], []


def run_plane(made, started):
    first, relays = made
    for i, relay in enumerate(relays):
        first[i].wait_recv()
        relay.start()
    started += first + relays
    for copy in relays if relays else first:
        copy.wait_recv()


def parent_matrix(parents_ref, r):
    size = parents_ref.shape[1]
    row = lax.broadcasted_iota(jnp.int32, (size, 128), 0)
    lane = lax.broadcasted_iota(jnp.int32, (size, 128), 1)
    hot = jnp.zeros((size, 128), F32)
    for i in range(size):
        hot = jnp.where((row == i) & (lane == parents_ref[r, i]), 1.0, hot)
    return hot


def fetch_all(sem, *pairs):
    loads = [pltpu.make_async_copy(src, dst, sem.at[i]) for i, (src, dst) in enumerate(pairs)]
    for load in loads:
        load.start()
    return loads


def share_kernel(
    n, parents_ref, counts_ref, owner_ref, q_ref, kv_ref, resid_ref,
    out_ref, owners_ref, blocks, send_sem, recv_sem, parents_s, counts_s, owner_s, load_sem,
):
    depth, plane = layout(n)
    me, z, p, c = position(n)
    rows = out_ref.shape[0]
    qw, kw, half = q_ref.shape[1], kv_ref.shape[1], resid_ref.shape[1] // 2
    tail = qw + kw + half
    lane = lax.broadcasted_iota(jnp.int32, (rows, 128), 1)
    second = pl.ds(rows, rows)
    own_half = pl.ds(pl.multiple_of(c * half, 128), half)
    loads = fetch_all(
        load_sem,
        (parents_ref, parents_s),
        (counts_ref, counts_s),
        (owner_ref, owner_s),
        (q_ref.at[second], blocks.at[me, :, pl.ds(0, qw)]),
        (kv_ref.at[second], blocks.at[me, :, pl.ds(qw, kw)]),
        (resid_ref.at[second, own_half], blocks.at[me, :, pl.ds(qw + kw, half)]),
    )
    greet(n, False)
    for load in loads:
        load.wait()
    info = parent_matrix(parents_s, 1)
    info = jnp.where(lane == COUNT_LANE, counts_s[1].astype(F32), info)
    info = jnp.where(lane == OWNER_LANE, owner_s[0].astype(F32), info)
    blocks[me, :, tail:] = info.astype(BF16)
    line = line_copies(n, blocks, send_sem, recv_sem)
    for copy in line:
        copy.start()
    started = list(line)
    waiting = None
    for back in range(depth):
        if back:
            line[back - 1].wait_recv()
        made = plane_copies(n, blocks, back, send_sem, recv_sem)
        for copy in made[0]:
            copy.start()
        if waiting:
            run_plane(waiting, started)
        waiting = made
    run_plane(waiting, started)
    for copy in started:
        copy.wait_send()

    out_ref[...] = jnp.zeros_like(out_ref)

    def pick(j, carry):
        tags = blocks[j, :, tail:].astype(F32)
        owner = jnp.sum(jnp.where(lane == OWNER_LANE, tags, 0.0), axis=1, keepdims=True)
        owners_ref[pl.ds(j, 1), :] = jnp.broadcast_to(owner, (rows, 128))[:1].astype(jnp.int32)
        mine = (owner == me.astype(F32)).astype(F32)
        out_ref[...] = (out_ref[...].astype(F32) + blocks[j].astype(F32) * mine).astype(BF16)
        return carry

    lax.fori_loop(0, n, pick, 0)


def roll_lanes(x, shift):
    w = x.shape[1]
    shift %= w
    if shift == 0:
        return x
    return jnp.concatenate([x[:, w - shift :], x[:, : w - shift]], axis=1)


def reach_of(hot):
    size = hot.shape[0]
    row = lax.broadcasted_iota(jnp.int32, (size, size), 0)
    col = lax.broadcasted_iota(jnp.int32, (size, size), 1)
    reach = hot + (row == col).astype(F32)
    for _ in range(size.bit_length()):
        twice = jnp.dot(reach.astype(BF16), reach.astype(BF16), preferred_element_type=F32)
        reach = jnp.minimum(twice, 1.0)
    return reach


def attend_kernel(
    pb, parents_ref, counts_ref, leaf_ref, table_ref, len_ref, q_ref, kv_ref, resid_ref, far_ref,
    cache_ref, w_out_ref, proj_ref, accepted_ref, pages, w_out, query, acc, peak, total, sem, w_sem,
    parents_s, counts_s, leaf_s, table_s, len_s, q_v, kv_v, resid_v, load_sem,
):
    loads = fetch_all(
        load_sem,
        (table_ref, table_s), (len_ref, len_s), (parents_ref, parents_s), (counts_ref, counts_s),
        (leaf_ref, leaf_s), (q_ref, q_v), (kv_ref, kv_v), (resid_ref, resid_v),
    )
    loads[0].wait()
    loads[1].wait()
    parents_ref, counts_ref, leaf_ref, table_ref, len_ref = parents_s, counts_s, leaf_s, table_s, len_s
    q_ref, kv_ref, resid_ref = q_v, kv_v, resid_v
    size = parents_ref.shape[1]
    qw, kw, half = q_ref.shape[1], kv_ref.shape[1], resid_ref.shape[1] // 2
    width = kw // 2
    heads = width // HEAD_DIM
    tail = qw + kw + half
    page_len = cache_ref.shape[2]
    keys = pb * page_len
    c = lax.axis_index("mlp")
    blocks = [(len_ref[s] + keys - 1) // keys for s in range(2)]

    for s in range(2):

        def fetch(b, carry):
            for i in range(pb):
                pltpu.make_async_copy(
                    cache_ref.at[table_ref[s, b * pb + i]], pages.at[s, b, i], sem.at[s, b]
                ).start()
            return carry

        lax.fori_loop(0, blocks[s], fetch, 0)
    w_copy = pltpu.make_async_copy(w_out_ref, w_out, w_sem)
    w_copy.start()
    for load in loads[2:]:
        load.wait()

    row = lax.broadcasted_iota(jnp.int32, (size, size), 0)
    col = lax.broadcasted_iota(jnp.int32, (size, size), 1)
    lane = lax.broadcasted_iota(jnp.int32, (size, width), 1)
    tags = far_ref[:, tail:].astype(F32)
    near = [parent_matrix(parents_ref, s)[:, :size] for s in range(2)]
    far_hot = tags[:, :size]
    far_count = tags[:, COUNT_LANE : COUNT_LANE + 1]
    own_reach = [reach_of(hot) for hot in near]
    far_reach = reach_of(far_hot)

    before = (row < col).astype(BF16)
    for s in range(2):
        path = jnp.sum(jnp.where(row == leaf_ref[s], own_reach[s], 0.0), axis=0, keepdims=True)
        wide = jnp.broadcast_to(path, (size, size))
        ranks = jnp.dot(wide.astype(BF16), before, preferred_element_type=F32)
        select = jnp.where(ranks == row.astype(F32), wide, 0.0).astype(BF16)
        accepted_ref[s * size : (s + 1) * size, :] = jnp.dot(
            select, kv_ref[s * size : (s + 1) * size, :], preferred_element_type=F32
        ).astype(BF16)

    live = [
        jnp.where(col < counts_ref[0], own_reach[0], 0.0),
        jnp.where(col.astype(F32) < far_count, far_reach, 0.0),
    ]
    copies = GROUP * heads
    dims = (((1,), (1,)), ((), ()))
    for s in range(2):
        q_rows = (q_ref[:size, :] if s == 0 else far_ref[:, :qw]).astype(F32) * HEAD_DIM**-0.5
        parts = []
        for g in range(GROUP):
            for h in range(heads):
                piece = roll_lanes(q_rows[:, h * width : (h + 1) * width], (h - g) * HEAD_DIM)
                inside = (lane >= h * HEAD_DIM) & (lane < (h + 1) * HEAD_DIM)
                parts.append(jnp.where(inside, piece, 0.0))
        query[s] = jnp.concatenate(parts, axis=0).astype(BF16)
        draft = kv_ref[:size, :] if s == 0 else far_ref[:, qw : qw + kw]
        scores = lax.dot_general(query[s], draft[:, :width], dims, preferred_element_type=F32)
        open_ = jnp.concatenate([live[s]] * copies, axis=0) > 0.5
        scores = jnp.where(open_, scores, -1e30)
        top = jnp.max(scores, axis=1, keepdims=True)
        weights = jnp.where(open_, jnp.exp(scores - top), 0.0)
        peak[s] = jnp.broadcast_to(top, peak.shape[1:])
        total[s] = jnp.broadcast_to(jnp.sum(weights, axis=1, keepdims=True), total.shape[1:])
        acc[s] = jnp.dot(weights.astype(BF16), draft[:, width:], preferred_element_type=F32)

    for s in range(2):

        def step(b, carry):
            pltpu.make_async_copy(cache_ref.at[pl.ds(0, pb)], pages.at[s, b], sem.at[s, b]).wait()
            k = pages[s, b, :, 0].reshape(keys, width)
            v = pages[s, b, :, 1].reshape(keys, width)
            scores = lax.dot_general(query[s], k, dims, preferred_element_type=F32)
            places = b * keys + lax.broadcasted_iota(jnp.int32, scores.shape, 1)
            scores = jnp.where(places < len_ref[s], scores, -1e30)
            old = peak[s][:, :1]
            new = jnp.maximum(old, jnp.max(scores, axis=1, keepdims=True))
            weights = jnp.exp(scores - new)
            factor = jnp.exp(old - new)
            peak[s] = jnp.broadcast_to(new, peak.shape[1:])
            total[s] = total[s] * factor + jnp.sum(weights, axis=1, keepdims=True)
            acc[s] = acc[s] * factor + jnp.dot(weights.astype(BF16), v, preferred_element_type=F32)
            return carry

        lax.fori_loop(0, blocks[s], step, 0)

    done = []
    for s in range(2):
        result = acc[s] / total[s][:, :1]
        cols = []
        for h in range(heads):
            col_sum = jnp.zeros((size, width), F32)
            for g in range(GROUP):
                at = (g * heads + h) * size
                inside = (lane >= h * HEAD_DIM) & (lane < (h + 1) * HEAD_DIM)
                piece = jnp.where(inside, result[at : at + size], 0.0)
                col_sum = col_sum + roll_lanes(piece, (g - h) * HEAD_DIM)
            cols.append(col_sum)
        done.append(jnp.concatenate(cols, axis=1))
    attended = jnp.concatenate(done, axis=0).astype(BF16)
    w_copy.wait()
    proj_ref[...] = jnp.dot(attended, w_out[...], preferred_element_type=F32)
    mine = pl.ds(pl.multiple_of(c * half, 128), half)
    proj_ref[:size, mine] += resid_ref[:size, mine].astype(F32)
    proj_ref[size:, mine] += far_ref[:, qw + kw : tail].astype(F32)


def rms(values, gain):
    factor = lax.rsqrt(jnp.mean(values * values, axis=-1, keepdims=True) + EPS)
    return (values * factor * gain.astype(F32).reshape(1, -1)).astype(BF16)


def layer_kernel(
    n, owners_ref, proj_ref, gain_mid_ref, gain_next_ref, w_in_hbm, w_down_hbm, w_next_hbm,
    hidden_ref, qkv_ref,
    w_in, w_down, w_next, other, mixed, rows_all, part, pair, ready, plane_in, line_out, line_in, final,
    w_sem, swap_sem, send_sem, recv_sem, fwd_send, fwd_recv, pair_send, pair_recv, rs_send, rs_recv,
):
    depth, plane = layout(n)
    me, z, p, c = position(n)
    size = ready.shape[1]
    width = ready.shape[2]
    loads = [
        pltpu.make_async_copy(src, dst, w_sem.at[i])
        for i, (src, dst) in enumerate(((w_in_hbm, w_in), (w_down_hbm, w_down), (w_next_hbm, w_next)))
    ]
    for load in loads:
        load.start()
    greet(n, True)
    partner = (me, 1 - c)
    swap = pltpu.make_async_remote_copy(
        proj_ref, other, swap_sem.at[0], swap_sem.at[1], device_id=partner, device_id_type=MESH
    )
    swap.start()
    swap.wait()
    both = (proj_ref[...] + other[...]).astype(BF16)
    mixed[0] = both[:size]
    mixed[1] = both[size:]
    mine = rows_all.at[c]
    rows_all[c, me] = rms(mixed[c].astype(F32), gain_mid_ref[...])

    line = line_copies(n, mine, send_sem, recv_sem)
    for copy in line:
        copy.start()
    def forward(back):
        group = pl.ds(lax.rem(z - back + depth, depth) * plane, plane)
        return pltpu.make_async_remote_copy(
            rows_all.at[c, group], rows_all.at[c, group],
            fwd_send.at[back], fwd_recv.at[back], device_id=partner, device_id_type=MESH,
        )

    def give(back):
        group = pl.ds(lax.rem(z - back + depth, depth) * plane, plane)
        return pltpu.make_async_remote_copy(
            part.at[1 - c, group], pair.at[group],
            pair_send.at[back], pair_recv.at[back], device_id=partner, device_id_type=MESH,
        )

    dims = (((1,), (1,)), ((), ()))

    def feed(back):
        forward(back).wait_recv()
        group = pl.ds(lax.rem(z - back + depth, depth) * plane, plane)
        x = rows_all[:, group].reshape(2 * plane * size, width)
        gate = lax.dot_general(x, w_in[0], dims, preferred_element_type=F32)
        up = lax.dot_general(x, w_in[1], dims, preferred_element_type=F32)
        hidden = (gate / (1.0 + jnp.exp(-gate)) * up).astype(BF16)
        y = jnp.dot(hidden, w_down[...], preferred_element_type=F32)
        part[:, group] = y.astype(BF16).reshape(2, plane, size, width)
        give(back).start()

    started = list(line)
    made = plane_copies(n, mine, 0, send_sem, recv_sem)
    for copy in made[0]:
        copy.start()
    for back in range(depth):
        waiting = made
        if back + 1 < depth:
            line[back].wait_recv()
            made = plane_copies(n, mine, back + 1, send_sem, recv_sem)
            for copy in made[0]:
                copy.start()
        run_plane(waiting, started)
        forward(back).start()
        if back == 0:
            loads[0].wait()
            loads[1].wait()
        else:
            feed(back - 1)
    feed(depth - 1)
    part[c, me] = (part[c, me].astype(F32) + mixed[c].astype(F32)).astype(BF16)
    for back in range(depth):
        give(back).wait_recv()

    def gather_row(e, carry):
        d = e + c * (owners_ref[e, 0] - e)
        ready[e] = (part[c, d].astype(F32) + pair[d].astype(F32)).astype(BF16)
        return carry

    lax.fori_loop(0, n, gather_row, 0)

    def to_plane(k, back):
        q = lax.rem(p + k, plane)
        i = (k - 1) * depth + back
        return pltpu.make_async_remote_copy(
            ready.at[lax.rem(z - back + depth, depth) * plane + q],
            plane_in.at[i],
            rs_send.at[i], rs_recv.at[i],
            device_id=(z * plane + q, c), device_id_type=MESH,
        )

    def to_line(back):
        i = (plane - 1) * depth + back
        return pltpu.make_async_remote_copy(
            line_out.at[back], line_in.at[back], rs_send.at[i], rs_recv.at[i],
            device_id=(lax.rem(z - back + depth, depth) * plane + p, c), device_id_type=MESH,
        )

    order = list(range(1, depth)) + [0]
    for back in order:
        for k in range(1, plane):
            to_plane(k, back).start()
    for back in order:
        for k in range(1, plane):
            to_plane(k, back).wait_recv()
        value = ready[lax.rem(z - back + depth, depth) * plane + p].astype(F32)
        for k in range(1, plane):
            value = value + plane_in[(k - 1) * depth + back].astype(F32)
        if back:
            line_out[back] = value.astype(BF16)
            to_line(back).start()
    for back in range(1, depth):
        to_line(back).wait_recv()
        value = value + line_in[back].astype(F32)
    final[c] = value.astype(BF16)
    last = pltpu.make_async_remote_copy(
        final.at[c], final.at[c], swap_sem.at[2], swap_sem.at[3], device_id=partner, device_id_type=MESH
    )
    last.start()
    loads[2].wait()
    last.wait()
    rows = jnp.concatenate([final[0], final[1]], axis=0)
    hidden_ref[...] = rows
    qkv_ref[...] = jnp.dot(
        rms(rows.astype(F32), gain_next_ref[...]), w_next[...], preferred_element_type=F32
    ).astype(BF16)
    for copy in started:
        copy.wait_send()
    for back in range(depth):
        forward(back).wait_send()
        give(back).wait_send()
        for k in range(1, plane):
            to_plane(k, back).wait_send()
        if back:
            to_line(back).wait_send()


def per_device(
    n, resid, q_in, kv_in, parents, counts, accept_leaf, cache, held_table, held_len, prev_owner,
    w_out, gain_mid, w_in, w_down, gain_next, w_next,
):
    depth, plane = layout(n)
    size = parents.shape[1]
    width = resid.shape[1]
    qw = q_in.shape[1]
    kw = 2 * kv_in.shape[2]
    kv = kv_in.reshape(2 * size, kw)
    block = qw + kw + width // 2 + 128
    smem = pl.BlockSpec(memory_space=pltpu.SMEM)
    vmem = pl.BlockSpec(memory_space=VMEM)
    hbm = pl.BlockSpec(memory_space=pl.ANY)
    dma = pltpu.SemaphoreType.DMA

    def smem_of(array):
        return pltpu.SMEM(array.shape, array.dtype)

    sends = depth - 1 + depth * plane
    far, owners = pl.pallas_call(
        functools.partial(share_kernel, n),
        out_shape=(
            jax.ShapeDtypeStruct((size, block), BF16),
            jax.ShapeDtypeStruct((n, 128), jnp.int32),
        ),
        in_specs=[hbm] * 6,
        out_specs=(vmem, vmem),
        scratch_shapes=[
            VMEM((n, size, block), BF16), dma((sends,)), dma((sends,)),
            smem_of(parents), smem_of(counts), smem_of(prev_owner), dma((6,)),
        ],
        compiler_params=pltpu.CompilerParams(
            collective_id=0, has_side_effects=True, vmem_limit_bytes=60 << 20
        ),
        name="share",
    )(parents, counts, prev_owner, q_in, kv, resid)

    pb = 4
    num_blocks = held_table.shape[1] // pb
    query_rows = size * qw // HEAD_DIM
    proj, accepted = pl.pallas_call(
        functools.partial(attend_kernel, pb),
        out_shape=(
            jax.ShapeDtypeStruct((2 * size, width), F32),
            jax.ShapeDtypeStruct((2 * size, kw), BF16),
        ),
        in_specs=[hbm] * 8 + [vmem] + [hbm] * 2,
        out_specs=(vmem, vmem),
        scratch_shapes=[
            VMEM((2, num_blocks, pb) + cache.shape[1:], BF16),
            VMEM(w_out.shape, BF16),
            VMEM((2, query_rows, kw // 2), BF16),
            VMEM((2, query_rows, kw // 2), F32),
            VMEM((2, query_rows, 128), F32),
            VMEM((2, query_rows, 128), F32),
            dma((2, num_blocks)),
            dma,
            smem_of(parents), smem_of(counts), smem_of(accept_leaf), smem_of(held_table), smem_of(held_len),
            VMEM(q_in.shape, BF16), VMEM(kv.shape, BF16), VMEM(resid.shape, BF16), dma((8,)),
        ],
        compiler_params=pltpu.CompilerParams(vmem_limit_bytes=60 << 20),
        name="attend",
    )(parents, counts, accept_leaf, held_table, held_len, q_in, kv, resid, far, cache, w_out)

    rows = (size, width)
    hidden_out, next_qkv = pl.pallas_call(
        functools.partial(layer_kernel, n),
        out_shape=(
            jax.ShapeDtypeStruct((2 * size, width), BF16),
            jax.ShapeDtypeStruct((2 * size, w_next.shape[1]), BF16),
        ),
        in_specs=[smem] + [vmem] * 3 + [hbm] * 3,
        out_specs=(vmem, vmem),
        scratch_shapes=[
            VMEM(w_in.shape, BF16),
            VMEM(w_down.shape, BF16),
            VMEM(w_next.shape, BF16),
            VMEM((2 * size, width), F32),
            VMEM((2,) + rows, BF16),
            VMEM((2, n) + rows, BF16),
            VMEM((2, n) + rows, BF16),
            VMEM((n,) + rows, BF16),
            VMEM((n,) + rows, BF16),
            VMEM(((plane - 1) * depth,) + rows, BF16),
            VMEM((depth,) + rows, BF16),
            VMEM((depth,) + rows, BF16),
            VMEM((2,) + rows, BF16),
            dma((3,)),
            dma((4,)),
            dma((sends,)),
            dma((sends,)),
            dma((depth,)),
            dma((depth,)),
            dma((depth,)),
            dma((depth,)),
            dma((plane * depth,)),
            dma((plane * depth,)),
        ],
        compiler_params=pltpu.CompilerParams(
            collective_id=1, has_side_effects=True, vmem_limit_bytes=60 << 20
        ),
        name="layer",
    )(
        owners, proj, gain_mid, gain_next,
        w_in, w_down, w_next,
    )
    return hidden_out, next_qkv, accepted.reshape(kv_in.shape)


def solution(mesh):
    placed = (
        P("req", None),
        P("req", "mlp"),
        P("req", None, "mlp"),
        P("req", None),
        P("req"),
        P("req"),
        P("req", None, None, "mlp"),
        P("req", None),
        P("req"),
        P("req"),
        P("mlp", None),
        P(),
        P(None, ("req", "mlp"), None),
        P(("req", "mlp"), None),
        P(),
        P(None, "mlp"),
    )
    return jax.shard_map(
        functools.partial(per_device, mesh.shape["req"]),
        mesh=mesh,
        in_specs=placed,
        out_specs=(P("req", None), P("req", "mlp"), P("req", None, "mlp")),
        check_vma=False,
    )
```

```python
import functools
import math

import jax
import jax.numpy as jnp
from jax import lax
from jax.experimental import pallas as pl
from jax.experimental.pallas import tpu as pltpu
from jax.sharding import PartitionSpec as P

HEAD_DIM = 64
GROUP = 4
EPS = 1e-05
MESH = pl.DeviceIdType.MESH
F32 = jnp.float32
BF16 = jnp.bfloat16
VMEM = pltpu.VMEM
OWNER_LANE = 65
COUNT_LANE = 64


def layout(n):
    depth = 4 if n % 4 == 0 else 1
    return depth, n // depth


def position(n):
    depth, plane = layout(n)
    me = lax.axis_index("req")
    return me, me // plane, lax.rem(me, plane), lax.axis_index("mlp")


def greet(n, partner):
    depth, plane = layout(n)
    me, z, p, c = position(n)
    barrier = pltpu.get_barrier_semaphore()
    peers = [(lax.rem(z + k, depth) * plane + p, c) for k in range(1, depth)]
    peers += [(z * plane + lax.rem(p + k, plane), c) for k in range(1, plane)]
    if partner:
        peers.append((me, 1 - c))
    for peer in peers:
        pl.semaphore_signal(barrier, inc=1, device_id=peer, device_id_type=MESH)
    pl.semaphore_wait(barrier, len(peers))


def line_copies(n, ref, send_sem, recv_sem):
    depth, plane = layout(n)
    me, z, p, c = position(n)
    made = []
    for k in range(1, depth):
        made.append(
            pltpu.make_async_remote_copy(
                ref.at[me],
                ref.at[me],
                send_sem.at[k - 1],
                recv_sem.at[k - 1],
                device_id=(lax.rem(z + k, depth) * plane + p, c),
                device_id_type=MESH,
            )
        )
    return made


def plane_copies(n, ref, back, send_sem, recv_sem):
    depth, plane = layout(n)
    me, z, p, c = position(n)
    base = lax.rem(z - back + depth, depth) * plane

    def copy(view, place, i):
        at = depth - 1 + back * plane + i
        return pltpu.make_async_remote_copy(
            view, view, send_sem.at[at], recv_sem.at[at],
            device_id=(z * plane + place, c), device_id_type=MESH,
        )

    return [copy(ref.at[base + p], lax.rem(p + k, plane), k - 1) for k in range(1, plane)], []


def run_plane(made, started):
    first, relays = made
    for i, relay in enumerate(relays):
        first[i].wait_recv()
        relay.start()
    started += first + relays
    for copy in relays if relays else first:
        copy.wait_recv()


def parent_matrix(parents_ref, r):
    size = parents_ref.shape[1]
    row = lax.broadcasted_iota(jnp.int32, (size, 128), 0)
    lane = lax.broadcasted_iota(jnp.int32, (size, 128), 1)
    hot = jnp.zeros((size, 128), F32)
    for i in range(size):
        hot = jnp.where((row == i) & (lane == parents_ref[r, i]), 1.0, hot)
    return hot


def fetch_all(sem, *pairs):
    loads = [pltpu.make_async_copy(src, dst, sem.at[i]) for i, (src, dst) in enumerate(pairs)]
    for load in loads:
        load.start()
    return loads


def share_kernel(
    n, parents_ref, counts_ref, owner_ref, q_ref, kv_ref, resid_ref,
    out_ref, owners_ref, blocks, send_sem, recv_sem, parents_s, counts_s, owner_s, load_sem,
):
    depth, plane = layout(n)
    me, z, p, c = position(n)
    rows = out_ref.shape[0]
    qw, kw, half = q_ref.shape[1], kv_ref.shape[1], resid_ref.shape[1] // 2
    tail = qw + kw + half
    lane = lax.broadcasted_iota(jnp.int32, (rows, 128), 1)
    second = pl.ds(rows, rows)
    own_half = pl.ds(pl.multiple_of(c * half, 128), half)
    loads = fetch_all(
        load_sem,
        (parents_ref, parents_s),
        (counts_ref, counts_s),
        (owner_ref, owner_s),
        (q_ref.at[second], blocks.at[me, :, pl.ds(0, qw)]),
        (kv_ref.at[second], blocks.at[me, :, pl.ds(qw, kw)]),
        (resid_ref.at[second, own_half], blocks.at[me, :, pl.ds(qw + kw, half)]),
    )
    greet(n, False)
    for load in loads:
        load.wait()
    info = parent_matrix(parents_s, 1)
    info = jnp.where(lane == COUNT_LANE, counts_s[1].astype(F32), info)
    info = jnp.where(lane == OWNER_LANE, owner_s[0].astype(F32), info)
    blocks[me, :, tail:] = info.astype(BF16)
    line = line_copies(n, blocks, send_sem, recv_sem)
    for copy in line:
        copy.start()
    started = list(line)
    waiting = None
    for back in range(depth):
        if back:
            line[back - 1].wait_recv()
        made = plane_copies(n, blocks, back, send_sem, recv_sem)
        for copy in made[0]:
            copy.start()
        if waiting:
            run_plane(waiting, started)
        waiting = made
    run_plane(waiting, started)
    for copy in started:
        copy.wait_send()

    out_ref[...] = jnp.zeros_like(out_ref)

    def pick(j, carry):
        tags = blocks[j, :, tail:].astype(F32)
        owner = jnp.sum(jnp.where(lane == OWNER_LANE, tags, 0.0), axis=1, keepdims=True)
        owners_ref[pl.ds(j, 1), :] = jnp.broadcast_to(owner, (rows, 128))[:1].astype(jnp.int32)
        mine = (owner == me.astype(F32)).astype(F32)
        out_ref[...] = (out_ref[...].astype(F32) + blocks[j].astype(F32) * mine).astype(BF16)
        return carry

    lax.fori_loop(0, n, pick, 0)


def roll_lanes(x, shift):
    w = x.shape[1]
    shift %= w
    if shift == 0:
        return x
    return jnp.concatenate([x[:, w - shift :], x[:, : w - shift]], axis=1)


def reach_of(hot):
    size = hot.shape[0]
    row = lax.broadcasted_iota(jnp.int32, (size, size), 0)
    col = lax.broadcasted_iota(jnp.int32, (size, size), 1)
    reach = hot + (row == col).astype(F32)
    for _ in range(size.bit_length()):
        twice = jnp.dot(reach.astype(BF16), reach.astype(BF16), preferred_element_type=F32)
        reach = jnp.minimum(twice, 1.0)
    return reach


def attend_kernel(
    pb, parents_ref, counts_ref, leaf_ref, table_ref, len_ref, q_ref, kv_ref, resid_ref, far_ref,
    cache_ref, w_out_ref, proj_ref, accepted_ref, pages, w_out, query, acc, peak, total, sem, w_sem,
    parents_s, counts_s, leaf_s, table_s, len_s, q_v, kv_v, resid_v, load_sem,
):
    loads = fetch_all(
        load_sem,
        (table_ref, table_s), (len_ref, len_s), (parents_ref, parents_s), (counts_ref, counts_s),
        (leaf_ref, leaf_s), (q_ref, q_v), (kv_ref, kv_v), (resid_ref, resid_v),
    )
    loads[0].wait()
    loads[1].wait()
    parents_ref, counts_ref, leaf_ref, table_ref, len_ref = parents_s, counts_s, leaf_s, table_s, len_s
    q_ref, kv_ref, resid_ref = q_v, kv_v, resid_v
    size = parents_ref.shape[1]
    qw, kw, half = q_ref.shape[1], kv_ref.shape[1], resid_ref.shape[1] // 2
    width = kw // 2
    heads = width // HEAD_DIM
    tail = qw + kw + half
    page_len = cache_ref.shape[2]
    keys = pb * page_len
    c = lax.axis_index("mlp")
    blocks = [(len_ref[s] + keys - 1) // keys for s in range(2)]

    for s in range(2):

        def fetch(b, carry):
            for i in range(pb):
                pltpu.make_async_copy(
                    cache_ref.at[table_ref[s, b * pb + i]], pages.at[s, b, i], sem.at[s, b]
                ).start()
            return carry

        lax.fori_loop(0, blocks[s], fetch, 0)
    w_copy = pltpu.make_async_copy(w_out_ref, w_out, w_sem)
    w_copy.start()
    for load in loads[2:]:
        load.wait()

    row = lax.broadcasted_iota(jnp.int32, (size, size), 0)
    col = lax.broadcasted_iota(jnp.int32, (size, size), 1)
    lane = lax.broadcasted_iota(jnp.int32, (size, width), 1)
    tags = far_ref[:, tail:].astype(F32)
    near = [parent_matrix(parents_ref, s)[:, :size] for s in range(2)]
    far_hot = tags[:, :size]
    far_count = tags[:, COUNT_LANE : COUNT_LANE + 1]
    own_reach = [reach_of(hot) for hot in near]
    far_reach = reach_of(far_hot)

    before = (row < col).astype(BF16)
    for s in range(2):
        path = jnp.sum(jnp.where(row == leaf_ref[s], own_reach[s], 0.0), axis=0, keepdims=True)
        wide = jnp.broadcast_to(path, (size, size))
        ranks = jnp.dot(wide.astype(BF16), before, preferred_element_type=F32)
        select = jnp.where(ranks == row.astype(F32), wide, 0.0).astype(BF16)
        accepted_ref[s * size : (s + 1) * size, :] = jnp.dot(
            select, kv_ref[s * size : (s + 1) * size, :], preferred_element_type=F32
        ).astype(BF16)

    live = [
        jnp.where(col < counts_ref[0], own_reach[0], 0.0),
        jnp.where(col.astype(F32) < far_count, far_reach, 0.0),
    ]
    copies = GROUP * heads
    dims = (((1,), (1,)), ((), ()))
    for s in range(2):
        q_rows = (q_ref[:size, :] if s == 0 else far_ref[:, :qw]).astype(F32) * HEAD_DIM**-0.5
        parts = []
        for g in range(GROUP):
            for h in range(heads):
                piece = roll_lanes(q_rows[:, h * width : (h + 1) * width], (h - g) * HEAD_DIM)
                inside = (lane >= h * HEAD_DIM) & (lane < (h + 1) * HEAD_DIM)
                parts.append(jnp.where(inside, piece, 0.0))
        query[s] = jnp.concatenate(parts, axis=0).astype(BF16)
        draft = kv_ref[:size, :] if s == 0 else far_ref[:, qw : qw + kw]
        scores = lax.dot_general(query[s], draft[:, :width], dims, preferred_element_type=F32)
        open_ = jnp.concatenate([live[s]] * copies, axis=0) > 0.5
        scores = jnp.where(open_, scores, -1e30)
        top = jnp.max(scores, axis=1, keepdims=True)
        weights = jnp.where(open_, jnp.exp(scores - top), 0.0)
        peak[s] = jnp.broadcast_to(top, peak.shape[1:])
        total[s] = jnp.broadcast_to(jnp.sum(weights, axis=1, keepdims=True), total.shape[1:])
        acc[s] = jnp.dot(weights.astype(BF16), draft[:, width:], preferred_element_type=F32)

    for s in range(2):

        def step(b, carry):
            pltpu.make_async_copy(cache_ref.at[pl.ds(0, pb)], pages.at[s, b], sem.at[s, b]).wait()
            k = pages[s, b, :, 0].reshape(keys, width)
            v = pages[s, b, :, 1].reshape(keys, width)
            scores = lax.dot_general(query[s], k, dims, preferred_element_type=F32)
            places = b * keys + lax.broadcasted_iota(jnp.int32, (1, keys), 1)
            scores = scores + jnp.where(places < len_ref[s], 0.0, -1e30)
            old = peak[s][:, :1]
            new = jnp.maximum(old, jnp.max(scores, axis=1, keepdims=True))
            weights = jnp.exp(scores - new)
            factor = jnp.exp(old - new)
            peak[s] = jnp.broadcast_to(new, peak.shape[1:])
            total[s] = total[s] * factor + jnp.sum(weights, axis=1, keepdims=True)
            acc[s] = acc[s] * factor + jnp.dot(weights.astype(BF16), v, preferred_element_type=F32)
            return carry

        lax.fori_loop(0, blocks[s], step, 0)

    done = []
    for s in range(2):
        result = acc[s] / total[s][:, :1]
        cols = []
        for h in range(heads):
            col_sum = jnp.zeros((size, width), F32)
            for g in range(GROUP):
                at = (g * heads + h) * size
                inside = (lane >= h * HEAD_DIM) & (lane < (h + 1) * HEAD_DIM)
                piece = jnp.where(inside, result[at : at + size], 0.0)
                col_sum = col_sum + roll_lanes(piece, (g - h) * HEAD_DIM)
            cols.append(col_sum)
        done.append(jnp.concatenate(cols, axis=1))
    attended = jnp.concatenate(done, axis=0).astype(BF16)
    w_copy.wait()
    proj_ref[...] = jnp.dot(attended, w_out[...], preferred_element_type=F32)
    mine = pl.ds(pl.multiple_of(c * half, 128), half)
    proj_ref[:size, mine] += resid_ref[:size, mine].astype(F32)
    proj_ref[size:, mine] += far_ref[:, qw + kw : tail].astype(F32)


def rms(values, gain):
    factor = lax.rsqrt(jnp.mean(values * values, axis=-1, keepdims=True) + EPS)
    return (values * factor * gain.astype(F32).reshape(1, -1)).astype(BF16)


def layer_kernel(
    n, owners_ref, proj_ref, gain_mid_ref, gain_next_ref, w_in_hbm, w_down_hbm, w_next_hbm,
    hidden_ref, qkv_ref,
    w_in, w_down, w_next, other, mixed, rows_all, part, pair, ready, plane_in, line_out, line_in, final,
    w_sem, swap_sem, send_sem, recv_sem, fwd_send, fwd_recv, pair_send, pair_recv, rs_send, rs_recv,
):
    depth, plane = layout(n)
    me, z, p, c = position(n)
    size = ready.shape[1]
    width = ready.shape[2]
    loads = [
        pltpu.make_async_copy(src, dst, w_sem.at[i])
        for i, (src, dst) in enumerate(((w_in_hbm, w_in), (w_down_hbm, w_down), (w_next_hbm, w_next)))
    ]
    for load in loads:
        load.start()
    greet(n, True)
    partner = (me, 1 - c)
    swap = pltpu.make_async_remote_copy(
        proj_ref, other, swap_sem.at[0], swap_sem.at[1], device_id=partner, device_id_type=MESH
    )
    swap.start()
    swap.wait()
    both = (proj_ref[...] + other[...]).astype(BF16)
    mixed[0] = both[:size]
    mixed[1] = both[size:]
    mine = rows_all.at[c]
    rows_all[c, me] = rms(mixed[c].astype(F32), gain_mid_ref[...])

    line = line_copies(n, mine, send_sem, recv_sem)
    for copy in line:
        copy.start()
    def forward(back):
        group = pl.ds(lax.rem(z - back + depth, depth) * plane, plane)
        return pltpu.make_async_remote_copy(
            rows_all.at[c, group], rows_all.at[c, group],
            fwd_send.at[back], fwd_recv.at[back], device_id=partner, device_id_type=MESH,
        )

    def give(back):
        group = pl.ds(lax.rem(z - back + depth, depth) * plane, plane)
        return pltpu.make_async_remote_copy(
            part.at[1 - c, group], pair.at[group],
            pair_send.at[back], pair_recv.at[back], device_id=partner, device_id_type=MESH,
        )

    dims = (((1,), (1,)), ((), ()))

    def feed(back):
        forward(back).wait_recv()
        group = pl.ds(lax.rem(z - back + depth, depth) * plane, plane)
        x = rows_all[:, group].reshape(2 * plane * size, width)
        gate = lax.dot_general(x, w_in[0], dims, preferred_element_type=F32)
        up = lax.dot_general(x, w_in[1], dims, preferred_element_type=F32)
        hidden = (gate / (1.0 + jnp.exp(-gate)) * up).astype(BF16)
        y = jnp.dot(hidden, w_down[...], preferred_element_type=F32)
        part[:, group] = y.astype(BF16).reshape(2, plane, size, width)
        give(back).start()

    started = list(line)
    made = plane_copies(n, mine, 0, send_sem, recv_sem)
    for copy in made[0]:
        copy.start()
    for back in range(depth):
        waiting = made
        if back + 1 < depth:
            line[back].wait_recv()
            made = plane_copies(n, mine, back + 1, send_sem, recv_sem)
            for copy in made[0]:
                copy.start()
        run_plane(waiting, started)
        forward(back).start()
        if back == 0:
            loads[0].wait()
            loads[1].wait()
        else:
            feed(back - 1)
    feed(depth - 1)
    part[c, me] = (part[c, me].astype(F32) + mixed[c].astype(F32)).astype(BF16)
    for back in range(depth):
        give(back).wait_recv()

    def gather_row(e, carry):
        d = e + c * (owners_ref[e, 0] - e)
        ready[e] = (part[c, d].astype(F32) + pair[d].astype(F32)).astype(BF16)
        return carry

    lax.fori_loop(0, n, gather_row, 0)

    def to_plane(k, back):
        q = lax.rem(p + k, plane)
        i = (k - 1) * depth + back
        return pltpu.make_async_remote_copy(
            ready.at[lax.rem(z - back + depth, depth) * plane + q],
            plane_in.at[i],
            rs_send.at[i], rs_recv.at[i],
            device_id=(z * plane + q, c), device_id_type=MESH,
        )

    def to_line(back):
        i = (plane - 1) * depth + back
        return pltpu.make_async_remote_copy(
            line_out.at[back], line_in.at[back], rs_send.at[i], rs_recv.at[i],
            device_id=(lax.rem(z - back + depth, depth) * plane + p, c), device_id_type=MESH,
        )

    order = list(range(1, depth)) + [0]
    for back in order:
        for k in range(1, plane):
            to_plane(k, back).start()
    for back in order:
        for k in range(1, plane):
            to_plane(k, back).wait_recv()
        value = ready[lax.rem(z - back + depth, depth) * plane + p].astype(F32)
        for k in range(1, plane):
            value = value + plane_in[(k - 1) * depth + back].astype(F32)
        if back:
            line_out[back] = value.astype(BF16)
            to_line(back).start()
    for back in range(1, depth):
        to_line(back).wait_recv()
        value = value + line_in[back].astype(F32)
    final[c] = value.astype(BF16)
    last = pltpu.make_async_remote_copy(
        final.at[c], final.at[c], swap_sem.at[2], swap_sem.at[3], device_id=partner, device_id_type=MESH
    )
    last.start()
    loads[2].wait()
    last.wait()
    rows = jnp.concatenate([final[0], final[1]], axis=0)
    hidden_ref[...] = rows
    qkv_ref[...] = jnp.dot(
        rms(rows.astype(F32), gain_next_ref[...]), w_next[...], preferred_element_type=F32
    ).astype(BF16)
    for copy in started:
        copy.wait_send()
    for back in range(depth):
        forward(back).wait_send()
        give(back).wait_send()
        for k in range(1, plane):
            to_plane(k, back).wait_send()
        if back:
            to_line(back).wait_send()


def per_device(
    n, resid, q_in, kv_in, parents, counts, accept_leaf, cache, held_table, held_len, prev_owner,
    w_out, gain_mid, w_in, w_down, gain_next, w_next,
):
    depth, plane = layout(n)
    size = parents.shape[1]
    width = resid.shape[1]
    qw = q_in.shape[1]
    kw = 2 * kv_in.shape[2]
    kv = kv_in.reshape(2 * size, kw)
    block = qw + kw + width // 2 + 128
    smem = pl.BlockSpec(memory_space=pltpu.SMEM)
    vmem = pl.BlockSpec(memory_space=VMEM)
    hbm = pl.BlockSpec(memory_space=pl.ANY)
    dma = pltpu.SemaphoreType.DMA

    def smem_of(array):
        return pltpu.SMEM(array.shape, array.dtype)

    sends = depth - 1 + depth * plane
    far, owners = pl.pallas_call(
        functools.partial(share_kernel, n),
        out_shape=(
            jax.ShapeDtypeStruct((size, block), BF16),
            jax.ShapeDtypeStruct((n, 128), jnp.int32),
        ),
        in_specs=[hbm] * 6,
        out_specs=(vmem, vmem),
        scratch_shapes=[
            VMEM((n, size, block), BF16), dma((sends,)), dma((sends,)),
            smem_of(parents), smem_of(counts), smem_of(prev_owner), dma((6,)),
        ],
        compiler_params=pltpu.CompilerParams(
            collective_id=0, has_side_effects=True, vmem_limit_bytes=60 << 20
        ),
        name="share",
    )(parents, counts, prev_owner, q_in, kv, resid)

    pb = math.gcd(held_table.shape[1], 8)
    num_blocks = held_table.shape[1] // pb
    query_rows = size * qw // HEAD_DIM
    proj, accepted = pl.pallas_call(
        functools.partial(attend_kernel, pb),
        out_shape=(
            jax.ShapeDtypeStruct((2 * size, width), F32),
            jax.ShapeDtypeStruct((2 * size, kw), BF16),
        ),
        in_specs=[hbm] * 8 + [vmem] + [hbm] * 2,
        out_specs=(vmem, vmem),
        scratch_shapes=[
            VMEM((2, num_blocks, pb) + cache.shape[1:], BF16),
            VMEM(w_out.shape, BF16),
            VMEM((2, query_rows, kw // 2), BF16),
            VMEM((2, query_rows, kw // 2), F32),
            VMEM((2, query_rows, 128), F32),
            VMEM((2, query_rows, 128), F32),
            dma((2, num_blocks)),
            dma,
            smem_of(parents), smem_of(counts), smem_of(accept_leaf), smem_of(held_table), smem_of(held_len),
            VMEM(q_in.shape, BF16), VMEM(kv.shape, BF16), VMEM(resid.shape, BF16), dma((8,)),
        ],
        compiler_params=pltpu.CompilerParams(vmem_limit_bytes=60 << 20),
        name="attend",
    )(parents, counts, accept_leaf, held_table, held_len, q_in, kv, resid, far, cache, w_out)

    rows = (size, width)
    hidden_out, next_qkv = pl.pallas_call(
        functools.partial(layer_kernel, n),
        out_shape=(
            jax.ShapeDtypeStruct((2 * size, width), BF16),
            jax.ShapeDtypeStruct((2 * size, w_next.shape[1]), BF16),
        ),
        in_specs=[smem] + [vmem] * 3 + [hbm] * 3,
        out_specs=(vmem, vmem),
        scratch_shapes=[
            VMEM(w_in.shape, BF16),
            VMEM(w_down.shape, BF16),
            VMEM(w_next.shape, BF16),
            VMEM((2 * size, width), F32),
            VMEM((2,) + rows, BF16),
            VMEM((2, n) + rows, BF16),
            VMEM((2, n) + rows, BF16),
            VMEM((n,) + rows, BF16),
            VMEM((n,) + rows, BF16),
            VMEM(((plane - 1) * depth,) + rows, BF16),
            VMEM((depth,) + rows, BF16),
            VMEM((depth,) + rows, BF16),
            VMEM((2,) + rows, BF16),
            dma((3,)),
            dma((4,)),
            dma((sends,)),
            dma((sends,)),
            dma((depth,)),
            dma((depth,)),
            dma((depth,)),
            dma((depth,)),
            dma((plane * depth,)),
            dma((plane * depth,)),
        ],
        compiler_params=pltpu.CompilerParams(
            collective_id=1, has_side_effects=True, vmem_limit_bytes=60 << 20
        ),
        name="layer",
    )(
        owners, proj, gain_mid, gain_next,
        w_in, w_down, w_next,
    )
    return hidden_out, next_qkv, accepted.reshape(kv_in.shape)


def solution(mesh):
    placed = (
        P("req", None),
        P("req", "mlp"),
        P("req", None, "mlp"),
        P("req", None),
        P("req"),
        P("req"),
        P("req", None, None, "mlp"),
        P("req", None),
        P("req"),
        P("req"),
        P("mlp", None),
        P(),
        P(None, ("req", "mlp"), None),
        P(("req", "mlp"), None),
        P(),
        P(None, "mlp"),
    )
    return jax.shard_map(
        functools.partial(per_device, mesh.shape["req"]),
        mesh=mesh,
        in_specs=placed,
        out_specs=(P("req", None), P("req", "mlp"), P("req", None, "mlp")),
        check_vma=False,
    )
```
